512 devices in a mesh: strip: 128 (over x, z, core), head: 4 (over y).
Axes of the slice: x: 4, y: 4, z: 16, core: 2. Of those that a mesh axis runs over, the one named last changes fastest.
Arguments:
- queries: bfloat16 [32768, 1024], P('strip', 'head'), may hold values from -40 to 40
- keys_in: bfloat16 [32768, 1024], P('strip', 'head'), may hold values from -40 to 40
- values_in: bfloat16 [32768, 1024], P('strip', 'head'), may hold values from -6 to 6
- grad_output: bfloat16 [32768, 1024], P('strip', 'head'), may hold values from -6 to 6
- w_output: bfloat16 [1024, 1024], P('head'), may hold values from -0.1875 to 0.1875
- link_dilation_index: int32 [256, 4], P('strip'), may hold values from 0 to 5, all different within a row
- clouds: int32 [256], P('strip'), may hold values 0 or 1
- edge_lengths: int32 [256], P('strip'), may hold values from 16 to 128
Outputs:
- attention_result: bfloat16 [32768, 1024], P('strip', 'head')
- grad_queries: bfloat16 [32768, 1024], P('strip', 'head')
- grad_keys: bfloat16 [32768, 1024], P('strip', 'head')
- grad_values: bfloat16 [32768, 1024], P('strip', 'head')
- grad_weight: float32 [1024, 1024], P('head')
The draws below stay inside these ranges and needn't reach their ends.
Inputs may be any that keep to these rules, and one draw needn't show every extreme that they name: `link_dilation_index`: each row names 4 different dilation steps.
All inputs are finite; a program needn't handle non-finite values. No bound on the sum of `clouds` on one device may be relied on, other than what follows from the above.
Results may differ from the reference program's by a relative error of at most 0.035.
Values may be sent and summed in bfloat16 or wider, within the bound.
A program may use at most 64 MiB of HBM per device.

```python
import jax
import jax.numpy as jnp
from jax import lax

D = 1024
HEADS = 16
HEAD_DIM = 64
BLOCK = 128
GROUPS = 2
STEP_COUNT = 3
LINKS = 4
DILATION_WIDTH = 16
TOKENS = 32768
N_STRIP = 128


def drawn_pair(key):
    base_keys = jax.random.truncated_normal(jax.random.fold_in(key, 11), -6.0, 6.0, (TOKENS, D), jnp.float32)
    home_query_rows = jax.random.truncated_normal(jax.random.fold_in(key, 12), -6.0, 6.0, (TOKENS, D), jnp.float32)
    return (home_query_rows, base_keys)


def draw_queries(key, part):
    return drawn_pair(key)[0].astype(jnp.bfloat16)


def draw_keys_in(key, part):
    return drawn_pair(key)[1].astype(jnp.bfloat16)


def with_ends(array, key, smallest, top_value):
    index_at = [jax.random.randint(jax.random.fold_in(key, axis), (), 0, length) for axis, length in enumerate(array.shape)]
    longest = array.shape.index(max(array.shape))
    next_to = index_at[:longest] + [(index_at[longest] + 1) % array.shape[longest]] + index_at[longest + 1:]
    return array.at[tuple(index_at)].set(smallest).at[tuple(next_to)].set(top_value)


def levels(rng, shape, pieces, least, high):
    factor_of, own = 1.0, jax.random.fold_in(rng, 6)
    for dim, parts in pieces:
        steps = jnp.exp(jax.random.uniform(jax.random.fold_in(own, dim), (parts,), jnp.float32, least / len(pieces), high / len(pieces)))
        factor_of = factor_of * jnp.repeat(steps, shape[dim] // parts).reshape([-1 if axis == dim else 1 for axis in range(len(shape))])
    return factor_of


def choose_distinct(own_key, rows, amount, top, lift):
    order = jax.random.permutation(jax.random.fold_in(own_key, 1), amount)
    favour = order
    for power in range(3):
        favour = favour * favour // amount
    favour = favour * lift // amount
    tickets = jax.random.randint(jax.random.fold_in(own_key, 2), (rows, amount), 0, 4096) + favour
    sure = jax.random.permutation(jax.random.fold_in(own_key, 3), rows)[jnp.arange(amount) % rows]
    tickets = jnp.where(jnp.arange(rows)[:, None] == sure[None, :], 1 << 14, tickets)
    priority = tickets * amount + jnp.arange(amount)
    return lax.top_k(priority.astype(jnp.int32), top)[1].astype(jnp.int32)


def normal_values(key, dims, spread, reach, shards=(), kind=jnp.bfloat16):
    result = jax.random.normal(key, dims, jnp.float32) * spread
    if len(shards) > 0:
        result = levels(key, dims, shards, -0.22, 0.18) * result
    return jnp.clip(result, min=-reach, max=reach).astype(kind)


def setup_inputs(seed: int = 0) -> dict:
    arg_keys = jax.random.split(jax.random.key(seed), 9)
    return {
        "queries": draw_queries(jax.random.fold_in(arg_keys[8], 71), 0),
        "keys_in": draw_keys_in(jax.random.fold_in(arg_keys[8], 71), 0),
        "values_in": normal_values(arg_keys[2], (TOKENS, D), 1.0, 6.0, ((0, 128), (1, 4))),
        "grad_output": normal_values(arg_keys[3], (TOKENS, D), 1.0, 6.0, ((0, 128), (1, 4))),
        "w_output": normal_values(arg_keys[4], (D, D), D ** -0.5, 0.1875, ((0, 4),)),
        "link_dilation_index": choose_distinct(arg_keys[5], (GROUPS * N_STRIP), 2 * STEP_COUNT, LINKS, 0),
        "clouds": with_ends((jax.random.randint(arg_keys[6], (GROUPS * N_STRIP,), 0, 4) < 1).astype(jnp.int32), jax.random.fold_in(arg_keys[6], 1), 0, 1),
        "edge_lengths": with_ends(jax.random.randint(arg_keys[7], (GROUPS * N_STRIP,), max(2, BLOCK // 8), BLOCK + 1), jax.random.fold_in(arg_keys[7], 1), max(2, BLOCK // 8), BLOCK).astype(jnp.int32),
    }


def block_tables(link_dilation_index, clouds, edge_lengths):
    block_count = GROUPS * N_STRIP
    blocks = jnp.arange(block_count, dtype=jnp.int32)
    strip_of = blocks // GROUPS
    group_of = blocks % GROUPS
    near_blocks = strip_of[:, None] * GROUPS + jnp.arange(GROUPS, dtype=jnp.int32)[None, :]
    near_live = (clouds[near_blocks] == 0) | (near_blocks == blocks[:, None])
    strip_offset = jnp.where(link_dilation_index < STEP_COUNT, DILATION_WIDTH * (link_dilation_index + 1), -DILATION_WIDTH * (link_dilation_index - STEP_COUNT + 1))
    target = strip_of[:, None] + strip_offset
    inside = (target >= 0) & (target < N_STRIP)
    far_blocks = (jnp.clip(target, 0, N_STRIP - 1) * GROUPS + group_of[:, None]).astype(jnp.int32)
    far_live = inside & (clouds[far_blocks] == 0)
    key_blocks = jnp.concatenate([near_blocks, far_blocks], axis=1).astype(jnp.int32)
    block_live = jnp.concatenate([near_live, far_live], axis=1)
    places = jnp.arange(BLOCK, dtype=jnp.int32)
    token_live = block_live[:, :, None] & (places[None, None, :] < edge_lengths[key_blocks][:, :, None])
    return key_blocks, token_live


def reference(queries, keys_in, values_in, grad_output, w_output, link_dilation_index, clouds, edge_lengths):
    block_count = GROUPS * N_STRIP
    slot_count = GROUPS + LINKS
    score_scale = HEAD_DIM ** -0.5
    key_blocks, token_live = block_tables(link_dilation_index, clouds, edge_lengths)
    head_shape = (block_count, BLOCK, HEADS, HEAD_DIM)
    query_heads = queries.reshape(head_shape)
    key_heads = keys_in.reshape(head_shape)
    value_heads = values_in.reshape(head_shape)
    grad_attn_all = jnp.dot(grad_output, w_output.T, preferred_element_type=jnp.float32).astype(jnp.bfloat16)
    grad_attn_all = grad_attn_all.reshape(head_shape)

    def strip_step(carry, strip_index):
        key_acc, value_acc = carry
        first = (strip_index * GROUPS).astype(jnp.int32)
        local_query = lax.dynamic_slice_in_dim(query_heads, first, GROUPS, 0)
        chosen = lax.dynamic_slice_in_dim(key_blocks, first, GROUPS, 0)
        live_keys = lax.dynamic_slice_in_dim(token_live, first, GROUPS, 0)
        local_grad = lax.dynamic_slice_in_dim(grad_attn_all, first, GROUPS, 0)
        gathered_keys = key_heads[chosen]
        gathered_values = value_heads[chosen]
        scores = jnp.einsum("gqhe,gkthe->ghqkt", local_query.astype(jnp.float32), gathered_keys.astype(jnp.float32)) * score_scale
        key_mask = live_keys[:, None, None, :, :]
        scores = jnp.where(key_mask, scores, -1e30)
        row_max = jnp.max(scores, axis=(3, 4), keepdims=True)
        weights = jnp.exp(scores - row_max)
        attention = weights / jnp.sum(weights, axis=(3, 4), keepdims=True)
        attention_low = attention.astype(jnp.bfloat16)
        attn = jnp.einsum("ghqkt,gkthe->gqhe", attention_low.astype(jnp.float32), gathered_values.astype(jnp.float32)).astype(jnp.bfloat16)
        correction = jnp.sum(local_grad.astype(jnp.float32) * attn.astype(jnp.float32), axis=3)
        correction = jnp.transpose(correction, (0, 2, 1))[:, :, :, None, None]
        grad_probs = jnp.einsum("gqhe,gkthe->ghqkt", local_grad.astype(jnp.float32), gathered_values.astype(jnp.float32))
        grad_scores = (attention * (grad_probs - correction)).astype(jnp.bfloat16)
        grad_query = (jnp.einsum("ghqkt,gkthe->gqhe", grad_scores.astype(jnp.float32), gathered_keys.astype(jnp.float32)) * score_scale).astype(jnp.bfloat16)
        key_terms = jnp.einsum("ghqkt,gqhe->gkthe", grad_scores.astype(jnp.float32), local_query.astype(jnp.float32)) * score_scale
        value_terms = jnp.einsum("ghqkt,gqhe->gkthe", attention_low.astype(jnp.float32), local_grad.astype(jnp.float32))
        flat_ids = chosen.reshape(-1)
        key_acc = key_acc.at[flat_ids].add(key_terms.reshape(GROUPS * slot_count, BLOCK, HEADS, HEAD_DIM))
        value_acc = value_acc.at[flat_ids].add(value_terms.reshape(GROUPS * slot_count, BLOCK, HEADS, HEAD_DIM))
        return (key_acc, value_acc), (attn, grad_query)

    zeros_acc = jnp.zeros(head_shape, jnp.float32)
    (key_acc, value_acc), (attn_parts, grad_query_parts) = lax.scan(strip_step, (zeros_acc, zeros_acc), jnp.arange(N_STRIP, dtype=jnp.int32))
    flat_shape = (block_count * BLOCK, HEADS * HEAD_DIM)
    attn = attn_parts.reshape(flat_shape)
    attention_result = jnp.dot(attn, w_output, preferred_element_type=jnp.float32).astype(jnp.bfloat16)
    grad_weight = jnp.dot(attn.T, grad_output, preferred_element_type=jnp.float32) * (block_count * BLOCK) ** -0.5
    grad_queries = grad_query_parts.reshape(flat_shape)
    grad_keys = key_acc.astype(jnp.bfloat16).reshape(flat_shape)
    grad_values = value_acc.astype(jnp.bfloat16).reshape(flat_shape)
    return (attention_result, grad_queries, grad_keys, grad_values, grad_weight)
```

```python
import functools
import math

import jax
import jax.numpy as jnp
from jax import lax
from jax.experimental import pallas as pl
from jax.experimental.pallas import tpu as pltpu
from jax.sharding import PartitionSpec as P

HEAD_DIM = 64
BLOCK = 128
HEADS = 4
FEAT = 256
TOK = 256
SLOTS = 8
NEG = -1e30
F32 = jnp.float32
BF16 = jnp.bfloat16
SCALE = HEAD_DIM**-0.5
SCALE2 = SCALE * math.log2(math.e)
MESH = pl.DeviceIdType.MESH

STEPS = ((2, 2), (-2, -2), (1, -1), (3, 1), (-1, -3), (-3, 3))
SLOT_X = (1, -1, 0, 1, -1, 2)


def link_of(step):
    return step - 1 if step > 0 else 2 - step


def nt(a, b):
    return lax.dot_general(a, b, (((1,), (1,)), ((), ())), preferred_element_type=F32)


def nn(a, b):
    return jnp.dot(a, b, preferred_element_type=F32)


def kernel(
    tokens,
    q_ref,
    k_ref,
    v_ref,
    go_ref,
    w_ref,
    link_ref,
    cloud_ref,
    edge_ref,
    out_ref,
    dq_ref,
    dk_ref,
    dv_ref,
    dw_ref,
    kv,
    qg,
    meta,
    stat,
    dof,
    wc,
    at,
    qb,
    gb,
    bias,
    nkv,
    s_buf,
    p_buf,
    low_buf,
    mcol,
    rcol,
    dcol,
    dk_acc,
    dv_acc,
    dwp,
    cs,
    cr,
    xs,
    xr,
    zf,
    zs,
    zr,
    gx,
    gc,
    send,
    recv,
):
    strip = lax.axis_index("strip")
    y = lax.axis_index("head")
    core = strip % 2
    z = (strip // 2) % 16
    x = strip // 32
    upper = z // 8

    def at_chip(dx, dz, other=0):
        c = (core + other) % 2
        return (((x + dx + 4) % 4) * 32 + ((z + dz) % 16) * 2 + c, y)

    def at_head(dy):
        return (strip, (y + dy) % 4)

    counter = [0]

    def copy(src, dst, device):
        i = counter[0]
        counter[0] += 1
        made = pltpu.make_async_remote_copy(
            src_ref=src,
            dst_ref=dst,
            send_sem=send.at[i],
            recv_sem=recv.at[i],
            device_id=device,
            device_id_type=MESH,
        )
        return made

    for g in range(2):
        for b in range(2):
            rows = pl.ds(b * BLOCK, BLOCK)
            kv[0, g, 6 + b] = k_ref[rows, :]
            kv[1, g, 6 + b] = v_ref[rows, :]
            qg[0, g, 6 + b] = q_ref[rows, :]
    dof[y] = go_ref[...]
    wc[y] = w_ref[:, pl.ds(pl.multiple_of(y * FEAT, FEAT), FEAT)]

    row_id = lax.broadcasted_iota(jnp.int32, (16, BLOCK), 0)
    mine = jnp.zeros((16, BLOCK), jnp.int32)
    member = []
    for g in range(2):
        live = jnp.where(cloud_ref[g] == 0, edge_ref[g], 0)
        mine = jnp.where(row_id == g, live, mine)
        row = []
        for l in range(6):
            has = jnp.int32(0)
            for n in range(4):
                has = has + jnp.where(link_ref[g, n] == l, 1, 0)
            row.append(has)
            mine = jnp.where(row_id == 2 + 6 * g + l, has, mine)
        member.append(row)
    meta[6] = mine

    peers = [at_chip(0, dz) for dz in range(1, 16)]
    peers += [at_chip(dx, 0) for dx in (1, 2, 3)]
    peers += [at_chip(dx, 8) for dx in (1, 2, 3)]
    peers += [at_head(dy) for dy in (1, 2, 3)]
    peers += [at_chip(0, 0, 1)]
    barrier = pltpu.get_barrier_semaphore()
    for peer in peers:
        pl.semaphore_signal(barrier, inc=1, device_id=peer, device_id_type=MESH)
    pl.semaphore_wait(barrier, len(peers))

    z_kv = [copy(kv.at[:, g, 6 + g], kv.at[:, g, 2], at_chip(0, 8)) for g in range(2)]
    z_qg = [copy(qg.at[:, g, 6 + g], qg.at[:, g, 2], at_chip(0, 8)) for g in range(2)]

    def own_plane(buf, g):
        return [
            copy(buf.at[:, g, 6 + g], buf.at[:, g, 1], at_chip(1, 0)),
            copy(buf.at[:, g, 6 + g], buf.at[:, g, 0], at_chip(-1, 0)),
        ]

    def onward(buf, g):
        return [
            copy(buf.at[:, g, 2], buf.at[:, g, 4], at_chip(1, 0)),
            copy(buf.at[:, g, 2], buf.at[:, g, 3], at_chip(-1, 0)),
            copy(buf.at[:, g, 2], buf.at[:, g, 5], at_chip(2, 0)),
        ]

    def to_far(buf):
        return [
            copy(buf.at[6], buf.at[1], at_chip(1, 0)),
            copy(buf.at[6], buf.at[0], at_chip(-1, 0)),
            copy(buf.at[6], buf.at[2], at_chip(0, 8)),
            copy(buf.at[6], buf.at[4], at_chip(1, 8)),
            copy(buf.at[6], buf.at[3], at_chip(-1, 8)),
            copy(buf.at[6], buf.at[5], at_chip(2, 8)),
        ]

    x_kv = [own_plane(kv, g) for g in range(2)]
    x_qg = [own_plane(qg, g) for g in range(2)]
    f_kv = [onward(kv, g) for g in range(2)]
    f_qg = [onward(qg, g) for g in range(2)]
    meta_out = to_far(meta)
    stat_out = to_far(stat)
    y_go = [copy(dof.at[y], dof.at[y], at_head(dy)) for dy in (1, 2, 3)]
    y_w = [
        copy(
            w_ref.at[:, pl.ds(pl.multiple_of((y + dy) % 4 * FEAT, FEAT), FEAT)],
            wc.at[y],
            at_head(dy),
        )
        for dy in (1, 2, 3)
    ]
    y_at = [copy(at.at[y], at.at[y], at_head(dy)) for dy in (1, 2, 3)]
    c_rs = copy(cs, cr, at_chip(0, 0, 1))
    x_rs = [copy(xs.at[(x + dx) % 4], xr.at[dx], at_chip(dx, 0)) for dx in (1, 2, 3)]
    x_ag = [copy(gx.at[x], gx.at[x], at_chip(dx, 0)) for dx in (1, 2, 3)]
    c_ag = copy(gx, gc, at_chip(0, 0, 1))
    base = counter[0]

    def z_rs(dz):
        return pltpu.make_async_remote_copy(
            src_ref=zs.at[(z + dz) % 16],
            dst_ref=zr.at[dz],
            send_sem=send.at[base + dz],
            recv_sem=recv.at[base + dz],
            device_id=at_chip(0, dz),
            device_id_type=MESH,
        )

    def z_ag(dz):
        return pltpu.make_async_remote_copy(
            src_ref=gx.at[x, z],
            dst_ref=gx.at[x, z],
            send_sem=send.at[base + 16 + dz],
            recv_sem=recv.at[base + 16 + dz],
            device_id=at_chip(0, dz),
            device_id_type=MESH,
        )

    def start(copies):
        for made in copies:
            made.start()

    def arrived(copies):
        for made in copies:
            made.wait_recv()

    def sent(copies):
        for made in copies:
            made.wait_send()

    start(y_go)
    start(z_kv[:1])
    start(x_kv[0])
    start(z_kv[1:])
    start(x_kv[1])
    start(meta_out)
    start(y_w)

    head_of = lax.broadcasted_iota(jnp.int32, (1, FEAT), 1) // HEAD_DIM
    in_head = [jnp.where(head_of == h, 1.0, 0.0).astype(F32) for h in range(HEADS)]
    in_head_low = [m.astype(BF16) for m in in_head]

    def spread(block):
        return jnp.concatenate([block * m for m in in_head_low], axis=0)

    def gathered(full):
        total = full[:BLOCK] * in_head[0]
        for h in range(1, HEADS):
            total = total + full[h * BLOCK : (h + 1) * BLOCK] * in_head[h]
        return total

    for g in range(2):
        qb[g] = spread(q_ref[g * BLOCK : (g + 1) * BLOCK, :])

    arrived(y_go)
    grad = nt(dof[0], w_ref[:, :FEAT])
    for i in range(1, 4):
        grad = grad + nt(dof[i], w_ref[:, i * FEAT : (i + 1) * FEAT])
    grad = grad.astype(BF16)
    for g in range(2):
        for b in range(2):
            qg[1, g, 6 + b] = grad[b * BLOCK : (b + 1) * BLOCK]
        gb[g] = spread(grad[g * BLOCK : (g + 1) * BLOCK])
    start(x_qg[0])
    start(x_qg[1])

    arrived(z_kv[:1])
    start(f_kv[0])
    start(z_qg)
    arrived(z_kv[1:])
    start(f_kv[1])

    arrived(meta_out)
    lane = lax.broadcasted_iota(jnp.int32, (1, BLOCK), 1)
    chain = 2 * x + upper
    for g in range(2):
        own_live = jnp.where(cloud_ref[g] == 0, edge_ref[g], 0)
        for j in range(6):
            far = meta[j]
            low_step, high_step = STEPS[j]
            step = jnp.where(upper == 0, low_step, high_step)
            inside = jnp.where((chain + step >= 0) & (chain + step < 8), 1, 0)
            listed = inside * jnp.where(
                upper == 0, member[g][link_of(low_step)], member[g][link_of(high_step)]
            )
            live = far[g : g + 1] * listed
            bias[g, :, j * BLOCK : (j + 1) * BLOCK] = jnp.where(lane < live, 0.0, NEG).astype(F32)
            here_low = 2 + 6 * g + link_of(-low_step)
            here_high = 2 + 6 * g + link_of(-high_step)
            lists_us = jnp.where(
                upper == 0, far[here_low : here_low + 1], far[here_high : here_high + 1]
            )
            nkv[g, j] = lists_us * (inside * own_live)
        for b in range(2):
            live = edge_ref[b] if b == g else jnp.where(cloud_ref[b] == 0, edge_ref[b], 0)
            bias[g, :, (6 + b) * BLOCK : (7 + b) * BLOCK] = jnp.where(lane < live, 0.0, NEG).astype(F32)
            nkv[b, 6 + g] = jnp.full((1, BLOCK), live, jnp.int32)

    CHUNK = 32

    def forward(g):
        keys = kv[0, g].reshape(SLOTS * BLOCK, FEAT)
        s_buf[...] = nt(qb[g], keys)

        def soft(r, _):
            rows = pl.ds(pl.multiple_of(r * CHUNK, CHUNK), CHUNK)
            s = s_buf[rows, :] * SCALE2 + bias[g]
            top = jnp.max(s, axis=1, keepdims=True)
            e = jnp.exp2(s - top)
            inv = 1.0 / jnp.sum(e, axis=1, keepdims=True)
            p = e * inv
            p_buf[g, rows, :] = p
            low_buf[rows, :] = p.astype(BF16)
            mcol[g, rows, :] = jnp.broadcast_to(top, (CHUNK, BLOCK))
            rcol[g, rows, :] = jnp.broadcast_to(inv, (CHUNK, BLOCK))
            return 0

        lax.fori_loop(0, HEADS * BLOCK // CHUNK, soft, 0)
        full = nn(low_buf[...], kv[1, g].reshape(SLOTS * BLOCK, FEAT))
        at[y, g * BLOCK : (g + 1) * BLOCK, :] = gathered(full).astype(BF16)

    for g in range(2):
        arrived(x_kv[g])
        arrived(f_kv[g])
        forward(g)

    start(y_at)
    attn_t = at[y].astype(F32).T.astype(BF16)
    weight_scale = tokens ** (-0.5)
    for i in range(4):
        dwp[i] = nn(attn_t, dof[i]) * weight_scale
    theirs = pl.ds(pl.multiple_of((1 - core) * BLOCK, BLOCK), BLOCK)
    ours = pl.ds(pl.multiple_of(core * BLOCK, BLOCK), BLOCK)
    for i in range(4):
        cs[i] = dwp[i, theirs, :].astype(BF16)
    c_rs.start()

    lane_full = lax.broadcasted_iota(jnp.int32, (BLOCK, BLOCK), 1)

    def correction(g):
        t = qg[1, g, 6 + g].astype(F32) * at[y, g * BLOCK : (g + 1) * BLOCK, :].astype(F32)
        packed = jnp.zeros((BLOCK, BLOCK), F32)
        for h in range(HEADS):
            rows = slice(h * BLOCK, (h + 1) * BLOCK)
            d = jnp.broadcast_to(jnp.sum(t * in_head[h], axis=1, keepdims=True), (BLOCK, BLOCK))
            dcol[rows, :] = d
            packed = jnp.where(lane_full == h, mcol[g, rows, :], packed)
            packed = jnp.where(lane_full == HEADS + h, rcol[g, rows, :], packed)
            packed = jnp.where(lane_full == 2 * HEADS + h, d, packed)
        stat[6, g] = packed.T[:16]

    def backward_queries(g):
        keys = kv[0, g].reshape(SLOTS * BLOCK, FEAT)
        s_buf[...] = nt(gb[g], kv[1, g].reshape(SLOTS * BLOCK, FEAT))

        def body(r, _):
            rows = pl.ds(pl.multiple_of(r * CHUNK, CHUNK), CHUNK)
            ds = p_buf[g, rows, :] * (s_buf[rows, :] - dcol[rows, 0:1])
            low_buf[rows, :] = ds.astype(BF16)
            return 0

        lax.fori_loop(0, HEADS * BLOCK // CHUNK, body, 0)
        full = nn(low_buf[...], keys)
        dq_ref[g * BLOCK : (g + 1) * BLOCK, :] = (gathered(full) * SCALE).astype(BF16)

    row_full = lax.broadcasted_iota(jnp.int32, (BLOCK, BLOCK), 0)

    def keys_step(g, j, slot, group):
        key, value = kv[0, g, 6 + g], kv[1, g, 6 + g]
        query, cot = spread(qg[0, g, j]), spread(qg[1, g, j])
        st = nt(key, query)
        dp = nt(value, cot)
        off = jnp.where(row_full < nkv[g, j], 0.0, NEG).astype(F32)
        rows = stat[slot, group]
        lows, ds = [], []
        for h in range(HEADS):
            cols = slice(h * BLOCK, (h + 1) * BLOCK)
            top = rows[h : h + 1]
            inv = rows[HEADS + h : HEADS + h + 1]
            d = rows[2 * HEADS + h : 2 * HEADS + h + 1]
            p = jnp.exp2(st[:, cols] * SCALE2 + off - top) * inv
            lows.append(p.astype(BF16))
            ds.append((p * (dp[:, cols] - d)).astype(BF16))
        dv_acc[g] += nn(jnp.concatenate(lows, axis=1), cot)
        dk_acc[g] += nn(jnp.concatenate(ds, axis=1), query)

    def keys_near(g):
        dv_acc[g] = jnp.zeros((BLOCK, FEAT), F32)
        dk_acc[g] = jnp.zeros((BLOCK, FEAT), F32)

        def body(b, _):
            keys_step(g, 6 + b, 6, b)
            return 0

        lax.fori_loop(0, 2, body, 0)

    def keys_far(g, first, last):
        def body(j, _):
            keys_step(g, j, j, g)
            return 0

        lax.fori_loop(first, last, body, 0)

    arrived(z_qg[:1])
    start(f_qg[0])
    correction(0)
    backward_queries(0)

    c_rs.wait_recv()
    for i in range(4):
        xs[i] = (dwp[i, ours, :] + cr[i].astype(F32)).astype(BF16)
    start(x_rs)
    correction(1)
    start(stat_out)
    backward_queries(1)
    arrived(z_qg[1:])
    start(f_qg[1])

    arrived(x_rs)
    part = dwp[x, ours, :] + cr[x].astype(F32)
    for dx in (1, 2, 3):
        part = part + xr[dx].astype(F32)
    for i in range(16):
        piece = part[i // 2 * 16 : i // 2 * 16 + 16, i % 2 * 128 : i % 2 * 128 + 128]
        zf[i] = piece
        zs[i] = piece.astype(BF16)

    def each_z(act):
        def body(dz, _):
            act(dz)
            return 0

        lax.fori_loop(1, 16, body, 0)

    each_z(lambda dz: z_rs(dz).start())

    arrived(y_at)
    arrived(y_w)
    result = nn(at[0], wc[0])
    for i in range(1, 4):
        result = result + nn(at[i], wc[i])
    out_ref[...] = result.astype(BF16)

    for g in range(2):
        keys_near(g)

    each_z(lambda dz: z_rs(dz).wait_recv())
    total = zf[z]
    for dz in range(1, 16):
        total = total + zr[dz].astype(F32)
    gx[x, z] = total.astype(BF16)
    each_z(lambda dz: z_ag(dz).start())

    arrived(stat_out)
    for g in range(2):
        arrived(x_qg[g])
        keys_far(g, 0, 2)

    each_z(lambda dz: z_ag(dz).wait_recv())
    start(x_ag)
    arrived(f_qg[0])
    keys_far(0, 2, 6)
    arrived(x_ag)
    c_ag.start()
    arrived(f_qg[1])
    keys_far(1, 2, 6)
    for g in range(2):
        rows = slice(g * BLOCK, (g + 1) * BLOCK)
        dk_ref[rows, :] = (dk_acc[g] * SCALE).astype(BF16)
        dv_ref[rows, :] = dv_acc[g].astype(BF16)

    def assemble(buf, first_row):
        def body(i, _):
            for n in range(16):
                rows = pl.ds(pl.multiple_of(first_row + n // 2 * 16, 16), 16)
                cols = pl.ds(pl.multiple_of(i * FEAT + n % 2 * 128, 128), 128)
                dw_ref[rows, cols] = buf[i, n].astype(F32)
            return 0

        lax.fori_loop(0, 4, body, 0)

    assemble(gx, core * BLOCK)
    c_ag.wait_recv()
    assemble(gc, (1 - core) * BLOCK)

    for copies in (z_kv, z_qg, *x_kv, *x_qg, *f_kv, *f_qg, meta_out, stat_out, y_go, y_w, y_at):
        sent(copies)
    sent([c_rs, *x_rs, *x_ag, c_ag])
    each_z(lambda dz: z_rs(dz).wait_send())
    each_z(lambda dz: z_ag(dz).wait_send())


SEMAPHORES = 96


def on_device(
    queries, keys_in, values_in, grad_output, w_output, link_dilation_index, clouds, edge_lengths
):
    tokens = queries.shape[0] * lax.axis_size("strip")
    vmem = pl.BlockSpec(memory_space=pltpu.VMEM)
    smem = pl.BlockSpec(memory_space=pltpu.SMEM)
    block = jax.ShapeDtypeStruct((TOK, FEAT), BF16)
    return pl.pallas_call(
        functools.partial(kernel, tokens),
        out_shape=(block, block, block, block, jax.ShapeDtypeStruct((FEAT, 4 * FEAT), F32)),
        in_specs=[vmem] * 5 + [smem] * 3,
        out_specs=(vmem,) * 5,
        scratch_shapes=[
            pltpu.VMEM((2, 2, SLOTS, BLOCK, FEAT), BF16),
            pltpu.VMEM((2, 2, SLOTS, BLOCK, FEAT), BF16),
            pltpu.VMEM((7, 16, BLOCK), jnp.int32),
            pltpu.VMEM((7, 2, 16, BLOCK), F32),
            pltpu.VMEM((4, TOK, FEAT), BF16),
            pltpu.VMEM((4, FEAT, FEAT), BF16),
            pltpu.VMEM((4, TOK, FEAT), BF16),
            pltpu.VMEM((2, HEADS * BLOCK, FEAT), BF16),
            pltpu.VMEM((2, HEADS * BLOCK, FEAT), BF16),
            pltpu.VMEM((2, 1, SLOTS * BLOCK), F32),
            pltpu.VMEM((2, SLOTS, 1, BLOCK), jnp.int32),
            pltpu.VMEM((HEADS * BLOCK, SLOTS * BLOCK), F32),
            pltpu.VMEM((2, HEADS * BLOCK, SLOTS * BLOCK), F32),
            pltpu.VMEM((HEADS * BLOCK, SLOTS * BLOCK), BF16),
            pltpu.VMEM((2, HEADS * BLOCK, BLOCK), F32),
            pltpu.VMEM((2, HEADS * BLOCK, BLOCK), F32),
            pltpu.VMEM((HEADS * BLOCK, BLOCK), F32),
            pltpu.VMEM((2, BLOCK, FEAT), F32),
            pltpu.VMEM((2, BLOCK, FEAT), F32),
            pltpu.VMEM((4, FEAT, FEAT), F32),
            pltpu.VMEM((4, BLOCK, FEAT), BF16),
            pltpu.VMEM((4, BLOCK, FEAT), BF16),
            pltpu.VMEM((4, BLOCK, FEAT), BF16),
            pltpu.VMEM((4, BLOCK, FEAT), BF16),
            pltpu.VMEM((16, 16, 128), F32),
            pltpu.VMEM((16, 16, 128), BF16),
            pltpu.VMEM((16, 16, 128), BF16),
            pltpu.VMEM((4, 16, 16, 128), BF16),
            pltpu.VMEM((4, 16, 16, 128), BF16),
            pltpu.SemaphoreType.DMA((SEMAPHORES,)),
            pltpu.SemaphoreType.DMA((SEMAPHORES,)),
        ],
        compiler_params=pltpu.CompilerParams(
            collective_id=0, has_side_effects=True, vmem_limit_bytes=48 * 2**20
        ),
    )(queries, keys_in, values_in, grad_output, w_output, link_dilation_index, clouds, edge_lengths)


def solution(mesh):
    return jax.shard_map(
        on_device,
        mesh=mesh,
        in_specs=(
            P("strip", "head"),
            P("strip", "head"),
            P("strip", "head"),
            P("strip", "head"),
            P("head", None),
            P("strip", None),
            P("strip"),
            P("strip"),
        ),
        out_specs=(
            P("strip", "head"),
            P("strip", "head"),
            P("strip", "head"),
            P("strip", "head"),
            P("head", None),
        ),
        check_vma=False,
    )
```

```python
import functools
import math

import jax
import jax.numpy as jnp
from jax import lax
from jax.experimental import pallas as pl
from jax.experimental.pallas import tpu as pltpu
from jax.sharding import PartitionSpec as P

HEAD_DIM = 64
BLOCK = 128
HEADS = 4
FEAT = 256
TOK = 256
SLOTS = 8
NEG = -1e30
F32 = jnp.float32
BF16 = jnp.bfloat16
SCALE = HEAD_DIM**-0.5
SCALE2 = SCALE * math.log2(math.e)
MESH = pl.DeviceIdType.MESH

STEPS = ((2, 2), (-2, -2), (1, -1), (3, 1), (-1, -3), (-3, 3))
SLOT_X = (1, -1, 0, 1, -1, 2)


def link_of(step):
    return step - 1 if step > 0 else 2 - step


def nt(a, b):
    return lax.dot_general(a, b, (((1,), (1,)), ((), ())), preferred_element_type=F32)


def nn(a, b):
    return jnp.dot(a, b, preferred_element_type=F32)


def kernel(
    tokens,
    q_ref,
    k_ref,
    v_ref,
    go_ref,
    w_ref,
    link_ref,
    cloud_ref,
    edge_ref,
    out_ref,
    dq_ref,
    dk_ref,
    dv_ref,
    dw_ref,
    w_in,
    kv,
    qg,
    meta,
    stat,
    dof,
    wc,
    at,
    qb,
    gb,
    bias,
    nkv,
    s_buf,
    p_buf,
    low_buf,
    mcol,
    rcol,
    dcol,
    dk_acc,
    dv_acc,
    dwp,
    cs,
    cr,
    xs,
    xr,
    xf,
    zs,
    gx,
    gc,
    send,
    recv,
    local,
):
    strip = lax.axis_index("strip")
    y = lax.axis_index("head")
    core = strip % 2
    z = (strip // 2) % 16
    x = strip // 32
    upper = z // 8

    def at_chip(dx, dz, other=0):
        c = (core + other) % 2
        return (((x + dx + 4) % 4) * 32 + ((z + dz) % 16) * 2 + c, y)

    quad = z // 4

    def near(n):
        return (((x + n // 4) % 4) * 32 + (quad * 4 + (z + n % 4) % 4) * 2 + core, y)

    def near_piece(n):
        return (x + n // 4) % 4 * 4 + (z + n % 4) % 4

    def at_head(dy):
        return (strip, (y + dy) % 4)

    counter = [0]

    def copy(src, dst, device):
        i = counter[0]
        counter[0] += 1
        made = pltpu.make_async_remote_copy(
            src_ref=src,
            dst_ref=dst,
            send_sem=send.at[i],
            recv_sem=recv.at[i],
            device_id=device,
            device_id_type=MESH,
        )
        return made

    peers = [near(n) for n in range(1, 16)]
    peers += [at_chip(0, dz) for dz in (4, 8, 12)]
    peers += [at_chip(dx, 8) for dx in (1, 2, 3)]
    peers += [at_head(dy) for dy in (1, 2, 3)]
    peers += [at_chip(0, 0, 1)]
    barrier = pltpu.get_barrier_semaphore()
    for peer in peers:
        pl.semaphore_signal(barrier, inc=1, device_id=peer, device_id_type=MESH)

    my_columns = pl.ds(pl.multiple_of(y * FEAT, FEAT), FEAT)
    pair = pl.ds(6, 2)
    fills = [pltpu.make_async_copy(go_ref, dof.at[y], local.at[0])]
    fills += [pltpu.make_async_copy(w_ref, w_in, local.at[1])]
    fills += [pltpu.make_async_copy(w_ref.at[:, my_columns], wc.at[y], local.at[2])]
    for g in range(2):
        fills += [pltpu.make_async_copy(q_ref, qg.at[0, g, pair], local.at[3 + g])]
        fills += [pltpu.make_async_copy(k_ref, kv.at[0, g, pair], local.at[5 + g])]
        fills += [pltpu.make_async_copy(v_ref, kv.at[1, g, pair], local.at[7 + g])]
    for made in fills:
        made.start()

    row_id = lax.broadcasted_iota(jnp.int32, (16, BLOCK), 0)
    mine = jnp.zeros((16, BLOCK), jnp.int32)
    member = []
    for g in range(2):
        live = jnp.where(cloud_ref[g] == 0, edge_ref[g], 0)
        mine = jnp.where(row_id == g, live, mine)
        row = []
        for l in range(6):
            has = jnp.int32(0)
            for n in range(4):
                has = has + jnp.where(link_ref[g, n] == l, 1, 0)
            row.append(has)
            mine = jnp.where(row_id == 2 + 6 * g + l, has, mine)
        member.append(row)
    meta[6] = mine

    pl.semaphore_wait(barrier, len(peers))

    own_grad = qg.at[1, 0, pair]
    sources = (k_ref, v_ref, q_ref, own_grad)
    places = [kv.at[0], kv.at[1], qg.at[0], qg.at[1]]
    cross, own, onward = [], [], []
    for src, place in zip(sources, places):
        cross.append([[copy(src.at[g], place.at[g, 2], at_chip(0, 8))] for g in range(2)])
        own.append(
            [copy(src, place.at[:, 1], at_chip(1, 0)), copy(src, place.at[:, 0], at_chip(-1, 0))]
        )
        onward.append(
            [
                [
                    copy(place.at[g, 2], place.at[g, 4], at_chip(1, 0)),
                    copy(place.at[g, 2], place.at[g, 3], at_chip(-1, 0)),
                    copy(place.at[g, 2], place.at[g, 5], at_chip(2, 0)),
                ]
                for g in range(2)
            ]
        )

    def to_far(buf):
        return [
            copy(buf.at[6], buf.at[1], at_chip(1, 0)),
            copy(buf.at[6], buf.at[0], at_chip(-1, 0)),
            copy(buf.at[6], buf.at[2], at_chip(0, 8)),
            copy(buf.at[6], buf.at[4], at_chip(1, 8)),
            copy(buf.at[6], buf.at[3], at_chip(-1, 8)),
            copy(buf.at[6], buf.at[5], at_chip(2, 8)),
        ]

    meta_out = to_far(meta)
    stat_out = to_far(stat)
    y_go = [copy(go_ref, dof.at[y], at_head(dy)) for dy in (1, 2, 3)]
    y_w = [
        copy(
            w_ref.at[:, pl.ds(pl.multiple_of((y + dy) % 4 * FEAT, FEAT), FEAT)],
            wc.at[y],
            at_head(dy),
        )
        for dy in (1, 2, 3)
    ]
    y_at = [copy(at.at[y], at.at[y], at_head(dy)) for dy in (1, 2, 3)]
    c_rs = copy(cs, cr, at_chip(0, 0, 1))
    z_sum = [copy(zs.at[quad], zs.at[quad], at_chip(0, dz)) for dz in (4, 8, 12)]
    c_ag = copy(gx, gc, at_chip(0, 0, 1))
    base = counter[0]

    def near_rs(n):
        return pltpu.make_async_remote_copy(
            src_ref=xs.at[near_piece(n)],
            dst_ref=xr.at[n],
            send_sem=send.at[base + n],
            recv_sem=recv.at[base + n],
            device_id=near(n),
            device_id_type=MESH,
        )

    def near_ag(n):
        return pltpu.make_async_remote_copy(
            src_ref=gx.at[near_piece(0)],
            dst_ref=gx.at[near_piece(0)],
            send_sem=send.at[base + 16 + n],
            recv_sem=recv.at[base + 16 + n],
            device_id=near(n),
            device_id_type=MESH,
        )

    def start(copies):
        for made in copies:
            made.start()

    def arrived(copies):
        for made in copies:
            made.wait_recv()

    def sent(copies):
        for made in copies:
            made.wait_send()

    key, value, query, cot = range(4)
    for g in range(2):
        start(cross[key][g])
    for g in range(2):
        start(cross[value][g])
    start(y_go)
    start(meta_out)

    head_of = lax.broadcasted_iota(jnp.int32, (1, FEAT), 1) // HEAD_DIM
    in_head = [jnp.where(head_of == h, 1.0, 0.0).astype(F32) for h in range(HEADS)]
    in_head_low = [m.astype(BF16) for m in in_head]

    def spread(block):
        return jnp.concatenate([block * m for m in in_head_low], axis=0)

    def gathered(full):
        total = full[:BLOCK] * in_head[0]
        for h in range(1, HEADS):
            total = total + full[h * BLOCK : (h + 1) * BLOCK] * in_head[h]
        return total

    for made in fills:
        made.wait()
    for g in range(2):
        qb[g] = spread(qg[0, 0, 6 + g])

    arrived(y_go)
    grad = nt(dof[0], w_in[:, :FEAT])
    for i in range(1, 4):
        grad = grad + nt(dof[i], w_in[:, i * FEAT : (i + 1) * FEAT])
    grad = grad.astype(BF16)
    for g in range(2):
        for b in range(2):
            qg[1, g, 6 + b] = grad[b * BLOCK : (b + 1) * BLOCK]
        gb[g] = spread(grad[g * BLOCK : (g + 1) * BLOCK])
    start(own[key])
    start(own[value])

    def pass_on(t, g):
        arrived(cross[t][g])
        start(onward[t][g])

    for g in range(2):
        pass_on(key, g)
    for g in range(2):
        start(cross[query][g])

    arrived(meta_out)
    lane = lax.broadcasted_iota(jnp.int32, (1, BLOCK), 1)
    chain = 2 * x + upper
    for g in range(2):
        own_live = jnp.where(cloud_ref[g] == 0, edge_ref[g], 0)
        for j in range(6):
            far = meta[j]
            low_step, high_step = STEPS[j]
            step = jnp.where(upper == 0, low_step, high_step)
            inside = jnp.where((chain + step >= 0) & (chain + step < 8), 1, 0)
            listed = inside * jnp.where(
                upper == 0, member[g][link_of(low_step)], member[g][link_of(high_step)]
            )
            live = far[g : g + 1] * listed
            bias[g, :, j * BLOCK : (j + 1) * BLOCK] = jnp.where(lane < live, 0.0, NEG).astype(F32)
            here_low = 2 + 6 * g + link_of(-low_step)
            here_high = 2 + 6 * g + link_of(-high_step)
            lists_us = jnp.where(
                upper == 0, far[here_low : here_low + 1], far[here_high : here_high + 1]
            )
            nkv[g, j] = lists_us * (inside * own_live)
        for b in range(2):
            live = edge_ref[b] if b == g else jnp.where(cloud_ref[b] == 0, edge_ref[b], 0)
            bias[g, :, (6 + b) * BLOCK : (7 + b) * BLOCK] = jnp.where(lane < live, 0.0, NEG).astype(F32)
            nkv[b, 6 + g] = jnp.full((1, BLOCK), live, jnp.int32)

    CHUNK = 32

    def scores(g):
        keys = kv[0, g].reshape(SLOTS * BLOCK, FEAT)
        s_buf[...] = nt(qb[g], keys)

        def soft(r, _):
            rows = pl.ds(pl.multiple_of(r * CHUNK, CHUNK), CHUNK)
            s = s_buf[rows, :] * SCALE2 + bias[g]
            top = jnp.max(s, axis=1, keepdims=True)
            e = jnp.exp2(s - top)
            inv = 1.0 / jnp.sum(e, axis=1, keepdims=True)
            p = e * inv
            p_buf[g, rows, :] = p
            low_buf[g, rows, :] = p.astype(BF16)
            mcol[g, rows, :] = jnp.broadcast_to(top, (CHUNK, BLOCK))
            rcol[g, rows, :] = jnp.broadcast_to(inv, (CHUNK, BLOCK))
            return 0

        lax.fori_loop(0, HEADS * BLOCK // CHUNK, soft, 0)

    def values(g):
        full = nn(low_buf[g], kv[1, g].reshape(SLOTS * BLOCK, FEAT))
        at[y, g * BLOCK : (g + 1) * BLOCK, :] = gathered(full).astype(BF16)

    pass_on(value, 0)
    for g in range(2):
        start(cross[cot][g])
    pass_on(value, 1)
    start(y_w)
    start(own[query])
    start(own[cot])
    arrived(own[key])
    for g in range(2):
        arrived(onward[key][g])
        scores(g)
    arrived(own[value])
    for g in range(2):
        arrived(onward[value][g])
        values(g)

    start(y_at)
    attn_t = at[y].astype(F32).T.astype(BF16)
    weight_scale = tokens ** (-0.5)
    for i in range(4):
        dwp[i] = nn(attn_t, dof[i]) * weight_scale
    theirs = pl.ds(pl.multiple_of((1 - core) * BLOCK, BLOCK), BLOCK)
    ours = pl.ds(pl.multiple_of(core * BLOCK, BLOCK), BLOCK)
    for i in range(4):
        cs[i] = dwp[i, theirs, :].astype(BF16)
    c_rs.start()

    lane_full = lax.broadcasted_iota(jnp.int32, (BLOCK, BLOCK), 1)

    def correction(g):
        t = qg[1, g, 6 + g].astype(F32) * at[y, g * BLOCK : (g + 1) * BLOCK, :].astype(F32)
        packed = jnp.zeros((BLOCK, BLOCK), F32)
        for h in range(HEADS):
            rows = slice(h * BLOCK, (h + 1) * BLOCK)
            d = jnp.broadcast_to(jnp.sum(t * in_head[h], axis=1, keepdims=True), (BLOCK, BLOCK))
            dcol[g, rows, :] = d
            packed = jnp.where(lane_full == h, mcol[g, rows, :], packed)
            packed = jnp.where(lane_full == HEADS + h, rcol[g, rows, :], packed)
            packed = jnp.where(lane_full == 2 * HEADS + h, d, packed)
        stat[6, g] = packed.T[:16]

    def backward_queries(g):
        keys = kv[0, g].reshape(SLOTS * BLOCK, FEAT)
        s_buf[...] = nt(gb[g], kv[1, g].reshape(SLOTS * BLOCK, FEAT))

        def body(r, _):
            rows = pl.ds(pl.multiple_of(r * CHUNK, CHUNK), CHUNK)
            ds = p_buf[g, rows, :] * (s_buf[rows, :] - dcol[g, rows, 0:1])
            low_buf[g, rows, :] = ds.astype(BF16)
            return 0

        lax.fori_loop(0, HEADS * BLOCK // CHUNK, body, 0)
        full = nn(low_buf[g], keys)
        dq_ref[g] = (gathered(full) * SCALE).astype(BF16)

    row_full = lax.broadcasted_iota(jnp.int32, (BLOCK, BLOCK), 0)

    def keys_step(g, j, slot, group):
        queries, cots = spread(qg[0, g, j]), spread(qg[1, g, j])
        st = nt(kv[0, g, 6 + g], queries)
        dp = nt(kv[1, g, 6 + g], cots)
        off = jnp.where(row_full < nkv[g, j], 0.0, NEG).astype(F32)
        rows = stat[slot, group]
        lows, ds = [], []
        for h in range(HEADS):
            cols = slice(h * BLOCK, (h + 1) * BLOCK)
            top = rows[h : h + 1]
            inv = rows[HEADS + h : HEADS + h + 1]
            d = rows[2 * HEADS + h : 2 * HEADS + h + 1]
            p = jnp.exp2(st[:, cols] * SCALE2 + off - top) * inv
            lows.append(p.astype(BF16))
            ds.append((p * (dp[:, cols] - d)).astype(BF16))
        dv_acc[g] += nn(jnp.concatenate(lows, axis=1), cots)
        dk_acc[g] += nn(jnp.concatenate(ds, axis=1), queries)

    def keys_near(g):
        dv_acc[g] = jnp.zeros((BLOCK, FEAT), F32)
        dk_acc[g] = jnp.zeros((BLOCK, FEAT), F32)

        def body(b, _):
            keys_step(g, 6 + b, 6, b)
            return 0

        lax.fori_loop(0, 2, body, 0)

    def keys_far(g, first, last):
        def body(j, _):
            keys_step(g, j, j, g)
            return 0

        lax.fori_loop(first, last, body, 0)

    def each_near(act):
        def body(n, _):
            act(n)
            return 0

        lax.fori_loop(1, 16, body, 0)

    correction(0)
    correction(1)
    start(stat_out)
    c_rs.wait_recv()
    for i in range(4):
        part = dwp[i, ours, :] + cr[i].astype(F32)
        for r in range(4):
            piece = part[r * 32 : (r + 1) * 32]
            xf[4 * i + r] = piece
            xs[4 * i + r] = piece.astype(BF16)
    each_near(lambda n: near_rs(n).start())
    for g in range(2):
        pass_on(query, g)
    backward_queries(0)

    each_near(lambda n: near_rs(n).wait_recv())
    part = xf[near_piece(0)]
    for n in range(1, 16):
        part = part + xr[n].astype(F32)
    zs[quad] = part.astype(BF16)
    start(z_sum)
    for g in range(2):
        pass_on(cot, g)
    backward_queries(1)

    arrived(y_at)
    arrived(y_w)
    result = nn(at[0], wc[0])
    for i in range(1, 4):
        result = result + nn(at[i], wc[i])
    for b in range(2):
        out_ref[b] = result[b * BLOCK : (b + 1) * BLOCK].astype(BF16)

    arrived(z_sum)
    part = zs[0].astype(F32)
    for i in range(1, 4):
        part = part + zs[i].astype(F32)
    gx[near_piece(0)] = part.astype(BF16)
    each_near(lambda n: near_ag(n).start())

    for g in range(2):
        keys_near(g)
    arrived(stat_out)
    arrived(own[query])
    arrived(own[cot])
    for g in range(2):
        keys_far(g, 0, 2)
    each_near(lambda n: near_ag(n).wait_recv())
    c_ag.start()
    for g in range(2):
        arrived(onward[query][g])
        arrived(onward[cot][g])
        keys_far(g, 2, 6)
        dk_ref[g] = (dk_acc[g] * SCALE).astype(BF16)
        dv_ref[g] = dv_acc[g].astype(BF16)

    def assemble(buf, first_row):
        for i in range(4):
            for r in range(4):
                rows = pl.ds(pl.multiple_of(first_row + r * 32, 32), 32)
                dw_ref[rows, i * FEAT : (i + 1) * FEAT] = buf[4 * i + r].astype(F32)

    assemble(gx, core * BLOCK)
    c_ag.wait_recv()
    assemble(gc, (1 - core) * BLOCK)

    for t in range(4):
        for g in range(2):
            sent(cross[t][g])
            sent(onward[t][g])
        sent(own[t])
    for copies in (meta_out, stat_out, y_go, y_w, y_at, z_sum):
        sent(copies)
    c_rs.wait_send()
    c_ag.wait_send()
    each_near(lambda n: near_rs(n).wait_send())
    each_near(lambda n: near_ag(n).wait_send())


SEMAPHORES = 128


def on_device(
    queries, keys_in, values_in, grad_output, w_output, link_dilation_index, clouds, edge_lengths
):
    tokens = queries.shape[0] * lax.axis_size("strip")
    vmem = pl.BlockSpec(memory_space=pltpu.VMEM)
    smem = pl.BlockSpec(memory_space=pltpu.SMEM)
    shape = (2, BLOCK, FEAT)
    block = jax.ShapeDtypeStruct(shape, BF16)
    anywhere = pl.BlockSpec(memory_space=pl.ANY)
    result, dq, dk, dv, dw = pl.pallas_call(
        functools.partial(kernel, tokens),
        out_shape=(block, block, block, block, jax.ShapeDtypeStruct((FEAT, 4 * FEAT), F32)),
        in_specs=[anywhere] * 5 + [smem] * 3,
        out_specs=(vmem,) * 5,
        scratch_shapes=[
            pltpu.VMEM((FEAT, 4 * FEAT), BF16),
            pltpu.VMEM((2, 2, SLOTS, BLOCK, FEAT), BF16),
            pltpu.VMEM((2, 2, SLOTS, BLOCK, FEAT), BF16),
            pltpu.VMEM((7, 16, BLOCK), jnp.int32),
            pltpu.VMEM((7, 2, 16, BLOCK), F32),
            pltpu.VMEM((4, TOK, FEAT), BF16),
            pltpu.VMEM((4, FEAT, FEAT), BF16),
            pltpu.VMEM((4, TOK, FEAT), BF16),
            pltpu.VMEM((2, HEADS * BLOCK, FEAT), BF16),
            pltpu.VMEM((2, HEADS * BLOCK, FEAT), BF16),
            pltpu.VMEM((2, 1, SLOTS * BLOCK), F32),
            pltpu.VMEM((2, SLOTS, 1, BLOCK), jnp.int32),
            pltpu.VMEM((HEADS * BLOCK, SLOTS * BLOCK), F32),
            pltpu.VMEM((2, HEADS * BLOCK, SLOTS * BLOCK), F32),
            pltpu.VMEM((2, HEADS * BLOCK, SLOTS * BLOCK), BF16),
            pltpu.VMEM((2, HEADS * BLOCK, BLOCK), F32),
            pltpu.VMEM((2, HEADS * BLOCK, BLOCK), F32),
            pltpu.VMEM((2, HEADS * BLOCK, BLOCK), F32),
            pltpu.VMEM((2, BLOCK, FEAT), F32),
            pltpu.VMEM((2, BLOCK, FEAT), F32),
            pltpu.VMEM((4, FEAT, FEAT), F32),
            pltpu.VMEM((4, BLOCK, FEAT), BF16),
            pltpu.VMEM((4, BLOCK, FEAT), BF16),
            pltpu.VMEM((16, 32, FEAT), BF16),
            pltpu.VMEM((16, 32, FEAT), BF16),
            pltpu.VMEM((16, 32, FEAT), F32),
            pltpu.VMEM((4, 32, FEAT), BF16),
            pltpu.VMEM((16, 32, FEAT), BF16),
            pltpu.VMEM((16, 32, FEAT), BF16),
            pltpu.SemaphoreType.DMA((SEMAPHORES,)),
            pltpu.SemaphoreType.DMA((SEMAPHORES,)),
            pltpu.SemaphoreType.DMA((9,)),
        ],
        compiler_params=pltpu.CompilerParams(
            collective_id=0, has_side_effects=True, vmem_limit_bytes=60 * 2**20
        ),
    )(
        queries.reshape(shape),
        keys_in.reshape(shape),
        values_in.reshape(shape),
        grad_output,
        w_output,
        link_dilation_index,
        clouds,
        edge_lengths,
    )
    flat = (TOK, FEAT)
    return result.reshape(flat), dq.reshape(flat), dk.reshape(flat), dv.reshape(flat), dw


def solution(mesh):
    return jax.shard_map(
        on_device,
        mesh=mesh,
        in_specs=(
            P("strip", "head"),
            P("strip", "head"),
            P("strip", "head"),
            P("strip", "head"),
            P("head", None),
            P("strip", None),
            P("strip"),
            P("strip"),
        ),
        out_specs=(
            P("strip", "head"),
            P("strip", "head"),
            P("strip", "head"),
            P("strip", "head"),
            P("head", None),
        ),
        check_vma=False,
    )
```

```python
import functools
import math

import jax
import jax.numpy as jnp
from jax import lax
from jax.experimental import pallas as pl
from jax.experimental.pallas import tpu as pltpu
from jax.sharding import PartitionSpec as P

HEAD_DIM = 64
BLOCK = 128
HEADS = 4
FEAT = 256
TOK = 256
SLOTS = 8
NEG = -1e30
F32 = jnp.float32
BF16 = jnp.bfloat16
SCALE = HEAD_DIM**-0.5
SCALE2 = SCALE * math.log2(math.e)
MESH = pl.DeviceIdType.MESH

STEPS = ((2, 2), (-2, -2), (1, -1), (3, 1), (-1, -3), (-3, 3))
SLOT_X = (1, -1, 0, 1, -1, 2)


def link_of(step):
    return step - 1 if step > 0 else 2 - step


def nt(a, b):
    return lax.dot_general(a, b, (((1,), (1,)), ((), ())), preferred_element_type=F32)


def nn(a, b):
    return jnp.dot(a, b, preferred_element_type=F32)


def kernel(
    tokens,
    q_ref,
    k_ref,
    v_ref,
    go_ref,
    w_ref,
    link_ref,
    cloud_ref,
    edge_ref,
    out_ref,
    dq_ref,
    dk_ref,
    dv_ref,
    dw_ref,
    w_in,
    kv,
    qg,
    meta,
    stat,
    dof,
    wc,
    at,
    qb,
    gb,
    bias,
    nkv,
    s_buf,
    p_buf,
    low_buf,
    mcol,
    rcol,
    dcol,
    dk_acc,
    dv_acc,
    dwp,
    cs,
    cr,
    xs,
    xr,
    xf,
    zs,
    gx,
    gc,
    send,
    recv,
    local,
):
    strip = lax.axis_index("strip")
    y = lax.axis_index("head")
    core = strip % 2
    z = (strip // 2) % 16
    x = strip // 32
    upper = z // 8

    def at_chip(dx, dz, other=0):
        c = (core + other) % 2
        return (((x + dx + 4) % 4) * 32 + ((z + dz) % 16) * 2 + c, y)

    quad = z // 4

    def near(n):
        return (((x + n // 4) % 4) * 32 + (quad * 4 + (z + n % 4) % 4) * 2 + core, y)

    def near_piece(n):
        return (x + n // 4) % 4 * 4 + (z + n % 4) % 4

    def at_head(dy):
        return (strip, (y + dy) % 4)

    counter = [0]

    def copy(src, dst, device):
        i = counter[0]
        counter[0] += 1
        made = pltpu.make_async_remote_copy(
            src_ref=src,
            dst_ref=dst,
            send_sem=send.at[i],
            recv_sem=recv.at[i],
            device_id=device,
            device_id_type=MESH,
        )
        return made

    peers = [near(n) for n in range(1, 16)]
    peers += [at_chip(0, dz) for dz in (4, 8, 12)]
    peers += [at_chip(dx, 8) for dx in (1, 2, 3)]
    peers += [at_head(dy) for dy in (1, 2, 3)]
    peers += [at_chip(0, 0, 1)]
    barrier = pltpu.get_barrier_semaphore()
    for peer in peers:
        pl.semaphore_signal(barrier, inc=1, device_id=peer, device_id_type=MESH)

    my_columns = pl.ds(pl.multiple_of(y * FEAT, FEAT), FEAT)
    pair = pl.ds(6, 2)
    fills = [pltpu.make_async_copy(go_ref, dof.at[y], local.at[0])]
    fills += [pltpu.make_async_copy(w_ref, w_in, local.at[1])]
    fills += [pltpu.make_async_copy(w_ref.at[:, my_columns], wc.at[y], local.at[2])]
    for g in range(2):
        fills += [pltpu.make_async_copy(q_ref, qg.at[0, g, pair], local.at[3 + g])]
        fills += [pltpu.make_async_copy(k_ref, kv.at[0, g, pair], local.at[5 + g])]
        fills += [pltpu.make_async_copy(v_ref, kv.at[1, g, pair], local.at[7 + g])]
    for made in fills:
        made.start()

    row_id = lax.broadcasted_iota(jnp.int32, (16, BLOCK), 0)
    mine = jnp.zeros((16, BLOCK), jnp.int32)
    member = []
    for g in range(2):
        live = jnp.where(cloud_ref[g] == 0, edge_ref[g], 0)
        mine = jnp.where(row_id == g, live, mine)
        row = []
        for l in range(6):
            has = jnp.int32(0)
            for n in range(4):
                has = has + jnp.where(link_ref[g, n] == l, 1, 0)
            row.append(has)
            mine = jnp.where(row_id == 2 + 6 * g + l, has, mine)
        member.append(row)
    meta[6] = mine

    pl.semaphore_wait(barrier, len(peers))

    own_grad = qg.at[1, 0, pair]
    sources = (k_ref, v_ref, q_ref, own_grad)
    places = [kv.at[0], kv.at[1], qg.at[0], qg.at[1]]
    cross, own, onward = [], [], []
    for src, place in zip(sources, places):
        cross.append([[copy(src.at[g], place.at[g, 2], at_chip(0, 8))] for g in range(2)])
        own.append(
            [copy(src, place.at[:, 1], at_chip(1, 0)), copy(src, place.at[:, 0], at_chip(-1, 0))]
        )
        onward.append(
            [
                [
                    copy(place.at[g, 2], place.at[g, 4], at_chip(1, 0)),
                    copy(place.at[g, 2], place.at[g, 3], at_chip(-1, 0)),
                    copy(place.at[g, 2], place.at[g, 5], at_chip(2, 0)),
                ]
                for g in range(2)
            ]
        )

    def to_far(buf):
        return [
            copy(buf.at[6], buf.at[1], at_chip(1, 0)),
            copy(buf.at[6], buf.at[0], at_chip(-1, 0)),
            copy(buf.at[6], buf.at[2], at_chip(0, 8)),
            copy(buf.at[6], buf.at[4], at_chip(1, 8)),
            copy(buf.at[6], buf.at[3], at_chip(-1, 8)),
            copy(buf.at[6], buf.at[5], at_chip(2, 8)),
        ]

    meta_out = to_far(meta)
    stat_out = to_far(stat)
    y_go = [copy(go_ref, dof.at[y], at_head(dy)) for dy in (1, 2, 3)]
    y_w = [
        copy(
            w_ref.at[:, pl.ds(pl.multiple_of((y + dy) % 4 * FEAT, FEAT), FEAT)],
            wc.at[y],
            at_head(dy),
        )
        for dy in (1, 2, 3)
    ]
    y_at = [copy(at.at[y], at.at[y], at_head(dy)) for dy in (1, 2, 3)]
    c_rs = copy(cs, cr, at_chip(0, 0, 1))
    z_sum = [copy(zs.at[quad], zs.at[quad], at_chip(0, dz)) for dz in (4, 8, 12)]
    def quarter(dx):
        return pl.ds((x - dx + 4) % 4 * 4, 4)

    c_ag = [copy(gx.at[quarter(dx)], gc.at[quarter(dx)], at_chip(0, 0, 1)) for dx in range(4)]
    base = counter[0]

    def near_rs(n):
        return pltpu.make_async_remote_copy(
            src_ref=xs.at[near_piece(n)],
            dst_ref=xr.at[n],
            send_sem=send.at[base + n],
            recv_sem=recv.at[base + n],
            device_id=near(n),
            device_id_type=MESH,
        )

    def near_ag(n):
        return pltpu.make_async_remote_copy(
            src_ref=gx.at[near_piece(0)],
            dst_ref=gx.at[near_piece(0)],
            send_sem=send.at[base + 16 + n],
            recv_sem=recv.at[base + 16 + n],
            device_id=near(n),
            device_id_type=MESH,
        )

    def start(copies):
        for made in copies:
            made.start()

    def arrived(copies):
        for made in copies:
            made.wait_recv()

    def sent(copies):
        for made in copies:
            made.wait_send()

    key, value, query, cot = range(4)
    for g in range(2):
        start(cross[key][g])
    for g in range(2):
        start(cross[value][g])
    start(y_go)
    start(meta_out)

    head_of = lax.broadcasted_iota(jnp.int32, (1, FEAT), 1) // HEAD_DIM
    in_head = [jnp.where(head_of == h, 1.0, 0.0).astype(F32) for h in range(HEADS)]
    in_head_low = [m.astype(BF16) for m in in_head]

    def spread(block):
        return jnp.concatenate([block * m for m in in_head_low], axis=0)

    def gathered(full):
        total = full[:BLOCK] * in_head[0]
        for h in range(1, HEADS):
            total = total + full[h * BLOCK : (h + 1) * BLOCK] * in_head[h]
        return total

    for made in fills:
        made.wait()
    for g in range(2):
        qb[g] = spread(qg[0, 0, 6 + g])

    arrived(y_go)
    grad = nt(dof[0], w_in[:, :FEAT])
    for i in range(1, 4):
        grad = grad + nt(dof[i], w_in[:, i * FEAT : (i + 1) * FEAT])
    grad = grad.astype(BF16)
    for g in range(2):
        for b in range(2):
            qg[1, g, 6 + b] = grad[b * BLOCK : (b + 1) * BLOCK]
        gb[g] = spread(grad[g * BLOCK : (g + 1) * BLOCK])
    start(own[key])
    start(own[value])

    def pass_on(t, g):
        arrived(cross[t][g])
        start(onward[t][g])

    for g in range(2):
        pass_on(key, g)
    for g in range(2):
        start(cross[query][g])

    arrived(meta_out)
    lane = lax.broadcasted_iota(jnp.int32, (1, BLOCK), 1)
    chain = 2 * x + upper
    for g in range(2):
        own_live = jnp.where(cloud_ref[g] == 0, edge_ref[g], 0)
        for j in range(6):
            far = meta[j]
            low_step, high_step = STEPS[j]
            step = jnp.where(upper == 0, low_step, high_step)
            inside = jnp.where((chain + step >= 0) & (chain + step < 8), 1, 0)
            listed = inside * jnp.where(
                upper == 0, member[g][link_of(low_step)], member[g][link_of(high_step)]
            )
            live = far[g : g + 1] * listed
            bias[g, :, j * BLOCK : (j + 1) * BLOCK] = jnp.where(lane < live, 0.0, NEG).astype(F32)
            here_low = 2 + 6 * g + link_of(-low_step)
            here_high = 2 + 6 * g + link_of(-high_step)
            lists_us = jnp.where(
                upper == 0, far[here_low : here_low + 1], far[here_high : here_high + 1]
            )
            nkv[g, j] = lists_us * (inside * own_live)
        for b in range(2):
            live = edge_ref[b] if b == g else jnp.where(cloud_ref[b] == 0, edge_ref[b], 0)
            bias[g, :, (6 + b) * BLOCK : (7 + b) * BLOCK] = jnp.where(lane < live, 0.0, NEG).astype(F32)
            nkv[b, 6 + g] = jnp.full((1, BLOCK), live, jnp.int32)

    CHUNK = 32

    def scores(g):
        keys = kv[0, g].reshape(SLOTS * BLOCK, FEAT)
        s_buf[...] = nt(qb[g], keys)

        def soft(r, _):
            rows = pl.ds(pl.multiple_of(r * CHUNK, CHUNK), CHUNK)
            s = s_buf[rows, :] * SCALE2 + bias[g]
            top = jnp.max(s, axis=1, keepdims=True)
            e = jnp.exp2(s - top)
            inv = 1.0 / jnp.sum(e, axis=1, keepdims=True)
            p = e * inv
            p_buf[g, rows, :] = p
            low_buf[g, rows, :] = p.astype(BF16)
            mcol[g, rows, :] = jnp.broadcast_to(top, (CHUNK, BLOCK))
            rcol[g, rows, :] = jnp.broadcast_to(inv, (CHUNK, BLOCK))
            return 0

        lax.fori_loop(0, HEADS * BLOCK // CHUNK, soft, 0)

    def values(g):
        full = nn(low_buf[g], kv[1, g].reshape(SLOTS * BLOCK, FEAT))
        at[y, g * BLOCK : (g + 1) * BLOCK, :] = gathered(full).astype(BF16)

    pass_on(value, 0)
    for g in range(2):
        start(cross[cot][g])
    pass_on(value, 1)
    start(y_w)
    start(own[query])
    start(own[cot])
    arrived(own[key])
    for g in range(2):
        arrived(onward[key][g])
        scores(g)
    arrived(own[value])
    for g in range(2):
        arrived(onward[value][g])
        values(g)

    start(y_at)
    attn_t = at[y].astype(F32).T.astype(BF16)
    weight_scale = tokens ** (-0.5)
    for i in range(4):
        dwp[i] = nn(attn_t, dof[i]) * weight_scale
    theirs = pl.ds(pl.multiple_of((1 - core) * BLOCK, BLOCK), BLOCK)
    ours = pl.ds(pl.multiple_of(core * BLOCK, BLOCK), BLOCK)
    for i in range(4):
        cs[i] = dwp[i, theirs, :].astype(BF16)
    c_rs.start()

    lane_full = lax.broadcasted_iota(jnp.int32, (BLOCK, BLOCK), 1)

    def correction(g):
        t = qg[1, g, 6 + g].astype(F32) * at[y, g * BLOCK : (g + 1) * BLOCK, :].astype(F32)
        packed = jnp.zeros((BLOCK, BLOCK), F32)
        for h in range(HEADS):
            rows = slice(h * BLOCK, (h + 1) * BLOCK)
            d = jnp.broadcast_to(jnp.sum(t * in_head[h], axis=1, keepdims=True), (BLOCK, BLOCK))
            dcol[g, rows, :] = d
            packed = jnp.where(lane_full == h, mcol[g, rows, :], packed)
            packed = jnp.where(lane_full == HEADS + h, rcol[g, rows, :], packed)
            packed = jnp.where(lane_full == 2 * HEADS + h, d, packed)
        stat[6, g] = packed.T[:16]

    def backward_queries(g):
        keys = kv[0, g].reshape(SLOTS * BLOCK, FEAT)
        s_buf[...] = nt(gb[g], kv[1, g].reshape(SLOTS * BLOCK, FEAT))

        def body(r, _):
            rows = pl.ds(pl.multiple_of(r * CHUNK, CHUNK), CHUNK)
            ds = p_buf[g, rows, :] * (s_buf[rows, :] - dcol[g, rows, 0:1])
            low_buf[g, rows, :] = ds.astype(BF16)
            return 0

        lax.fori_loop(0, HEADS * BLOCK // CHUNK, body, 0)
        full = nn(low_buf[g], keys)
        dq_ref[g] = (gathered(full) * SCALE).astype(BF16)

    row_full = lax.broadcasted_iota(jnp.int32, (BLOCK, BLOCK), 0)

    def keys_step(g, j, slot, group):
        queries, cots = spread(qg[0, g, j]), spread(qg[1, g, j])
        st = nt(kv[0, g, 6 + g], queries)
        dp = nt(kv[1, g, 6 + g], cots)
        off = jnp.where(row_full < nkv[g, j], 0.0, NEG).astype(F32)
        rows = stat[slot, group]
        lows, ds = [], []
        for h in range(HEADS):
            cols = slice(h * BLOCK, (h + 1) * BLOCK)
            top = rows[h : h + 1]
            inv = rows[HEADS + h : HEADS + h + 1]
            d = rows[2 * HEADS + h : 2 * HEADS + h + 1]
            p = jnp.exp2(st[:, cols] * SCALE2 + off - top) * inv
            lows.append(p.astype(BF16))
            ds.append((p * (dp[:, cols] - d)).astype(BF16))
        dv_acc[g] += nn(jnp.concatenate(lows, axis=1), cots)
        dk_acc[g] += nn(jnp.concatenate(ds, axis=1), queries)

    def keys_near(g):
        dv_acc[g] = jnp.zeros((BLOCK, FEAT), F32)
        dk_acc[g] = jnp.zeros((BLOCK, FEAT), F32)

        def body(b, _):
            keys_step(g, 6 + b, 6, b)
            return 0

        lax.fori_loop(0, 2, body, 0)

    def keys_far(g, first, last):
        def body(j, _):
            keys_step(g, j, j, g)
            return 0

        lax.fori_loop(first, last, body, 0)

    def each_near(act):
        def body(n, _):
            act(n)
            return 0

        lax.fori_loop(1, 16, body, 0)

    correction(0)
    correction(1)
    start(stat_out)
    c_rs.wait_recv()
    for i in range(4):
        part = dwp[i, ours, :] + cr[i].astype(F32)
        for r in range(4):
            piece = part[r * 32 : (r + 1) * 32]
            xf[4 * i + r] = piece
            xs[4 * i + r] = piece.astype(BF16)
    each_near(lambda n: near_rs(n).start())
    for g in range(2):
        pass_on(query, g)
    backward_queries(0)

    each_near(lambda n: near_rs(n).wait_recv())
    part = xf[near_piece(0)]
    for n in range(1, 16):
        part = part + xr[n].astype(F32)
    zs[quad] = part.astype(BF16)
    start(z_sum)
    for g in range(2):
        pass_on(cot, g)
    backward_queries(1)

    arrived(y_at)
    arrived(y_w)
    result = nn(at[0], wc[0])
    for i in range(1, 4):
        result = result + nn(at[i], wc[i])
    for b in range(2):
        out_ref[b] = result[b * BLOCK : (b + 1) * BLOCK].astype(BF16)

    arrived(z_sum)
    part = zs[0].astype(F32)
    for i in range(1, 4):
        part = part + zs[i].astype(F32)
    gx[near_piece(0)] = part.astype(BF16)
    each_near(lambda n: near_ag(n).start())

    for g in range(2):
        keys_near(g)
    arrived(stat_out)
    arrived(own[query])
    arrived(own[cot])
    for g in range(2):
        keys_far(g, 0, 2)
    arrived(onward[query][0])
    arrived(onward[cot][0])
    keys_far(0, 2, 6)
    for dx in range(4):
        for n in range(max(1, 4 * dx), 4 * dx + 4):
            near_ag(n).wait_recv()
        c_ag[dx].start()
    for g in range(2):
        if g == 1:
            arrived(onward[query][g])
            arrived(onward[cot][g])
            keys_far(g, 2, 6)
        dk_ref[g] = (dk_acc[g] * SCALE).astype(BF16)
        dv_ref[g] = dv_acc[g].astype(BF16)

    def assemble(buf, first_row):
        for i in range(4):
            for r in range(4):
                rows = pl.ds(pl.multiple_of(first_row + r * 32, 32), 32)
                dw_ref[rows, i * FEAT : (i + 1) * FEAT] = buf[4 * i + r].astype(F32)

    assemble(gx, core * BLOCK)
    arrived(c_ag)
    assemble(gc, (1 - core) * BLOCK)

    for t in range(4):
        for g in range(2):
            sent(cross[t][g])
            sent(onward[t][g])
        sent(own[t])
    for copies in (meta_out, stat_out, y_go, y_w, y_at, z_sum):
        sent(copies)
    c_rs.wait_send()
    sent(c_ag)
    each_near(lambda n: near_rs(n).wait_send())
    each_near(lambda n: near_ag(n).wait_send())


SEMAPHORES = 128


def hand_over(*refs):
    for src, dst in zip(refs[:5], refs[5:]):
        dst[...] = src[...]


def on_device(
    queries, keys_in, values_in, grad_output, w_output, link_dilation_index, clouds, edge_lengths
):
    tokens = queries.shape[0] * lax.axis_size("strip")
    vmem = pl.BlockSpec(memory_space=pltpu.VMEM)
    smem = pl.BlockSpec(memory_space=pltpu.SMEM)
    shape = (2, BLOCK, FEAT)
    block = jax.ShapeDtypeStruct(shape, BF16)
    anywhere = pl.BlockSpec(memory_space=pl.ANY)
    parts = pl.pallas_call(
        functools.partial(kernel, tokens),
        out_shape=(block, block, block, block, jax.ShapeDtypeStruct((FEAT, 4 * FEAT), F32)),
        in_specs=[anywhere] * 5 + [smem] * 3,
        out_specs=(vmem,) * 5,
        scratch_shapes=[
            pltpu.VMEM((FEAT, 4 * FEAT), BF16),
            pltpu.VMEM((2, 2, SLOTS, BLOCK, FEAT), BF16),
            pltpu.VMEM((2, 2, SLOTS, BLOCK, FEAT), BF16),
            pltpu.VMEM((7, 16, BLOCK), jnp.int32),
            pltpu.VMEM((7, 2, 16, BLOCK), F32),
            pltpu.VMEM((4, TOK, FEAT), BF16),
            pltpu.VMEM((4, FEAT, FEAT), BF16),
            pltpu.VMEM((4, TOK, FEAT), BF16),
            pltpu.VMEM((2, HEADS * BLOCK, FEAT), BF16),
            pltpu.VMEM((2, HEADS * BLOCK, FEAT), BF16),
            pltpu.VMEM((2, 1, SLOTS * BLOCK), F32),
            pltpu.VMEM((2, SLOTS, 1, BLOCK), jnp.int32),
            pltpu.VMEM((HEADS * BLOCK, SLOTS * BLOCK), F32),
            pltpu.VMEM((2, HEADS * BLOCK, SLOTS * BLOCK), F32),
            pltpu.VMEM((2, HEADS * BLOCK, SLOTS * BLOCK), BF16),
            pltpu.VMEM((2, HEADS * BLOCK, BLOCK), F32),
            pltpu.VMEM((2, HEADS * BLOCK, BLOCK), F32),
            pltpu.VMEM((2, HEADS * BLOCK, BLOCK), F32),
            pltpu.VMEM((2, BLOCK, FEAT), F32),
            pltpu.VMEM((2, BLOCK, FEAT), F32),
            pltpu.VMEM((4, FEAT, FEAT), F32),
            pltpu.VMEM((4, BLOCK, FEAT), BF16),
            pltpu.VMEM((4, BLOCK, FEAT), BF16),
            pltpu.VMEM((16, 32, FEAT), BF16),
            pltpu.VMEM((16, 32, FEAT), BF16),
            pltpu.VMEM((16, 32, FEAT), F32),
            pltpu.VMEM((4, 32, FEAT), BF16),
            pltpu.VMEM((16, 32, FEAT), BF16),
            pltpu.VMEM((16, 32, FEAT), BF16),
            pltpu.SemaphoreType.DMA((SEMAPHORES,)),
            pltpu.SemaphoreType.DMA((SEMAPHORES,)),
            pltpu.SemaphoreType.DMA((9,)),
        ],
        compiler_params=pltpu.CompilerParams(
            collective_id=0, has_side_effects=True, vmem_limit_bytes=60 * 2**20
        ),
    )(
        queries.reshape(shape),
        keys_in.reshape(shape),
        values_in.reshape(shape),
        grad_output,
        w_output,
        link_dilation_index,
        clouds,
        edge_lengths,
    )
    result, dq, dk, dv, dw = pl.pallas_call(
        hand_over,
        out_shape=[jax.ShapeDtypeStruct(part.shape, part.dtype) for part in parts],
        in_specs=[vmem] * 5,
        out_specs=[vmem] * 5,
    )(*parts)
    flat = (TOK, FEAT)
    return result.reshape(flat), dq.reshape(flat), dk.reshape(flat), dv.reshape(flat), dw


def solution(mesh):
    return jax.shard_map(
        on_device,
        mesh=mesh,
        in_specs=(
            P("strip", "head"),
            P("strip", "head"),
            P("strip", "head"),
            P("strip", "head"),
            P("head", None),
            P("strip", None),
            P("strip"),
            P("strip"),
        ),
        out_specs=(
            P("strip", "head"),
            P("strip", "head"),
            P("strip", "head"),
            P("strip", "head"),
            P("head", None),
        ),
        check_vma=False,
    )
```

```python
import functools
import math

import jax
import jax.numpy as jnp
from jax import lax
from jax.experimental import pallas as pl
from jax.experimental.pallas import tpu as pltpu
from jax.sharding import PartitionSpec as P

HEAD_DIM = 64
BLOCK = 128
HEADS = 4
FEAT = 256
TOK = 256
SLOTS = 8
NEG = -1e30
F32 = jnp.float32
BF16 = jnp.bfloat16
SCALE = HEAD_DIM**-0.5
SCALE2 = SCALE * math.log2(math.e)
MESH = pl.DeviceIdType.MESH

STEPS = ((2, 2), (-2, -2), (1, -1), (3, 1), (-1, -3), (-3, 3))
SLOT_X = (1, -1, 0, 1, -1, 2)


def link_of(step):
    return step - 1 if step > 0 else 2 - step


def nt(a, b):
    return lax.dot_general(a, b, (((1,), (1,)), ((), ())), preferred_element_type=F32)


def nn(a, b):
    return jnp.dot(a, b, preferred_element_type=F32)


def kernel(
    tokens,
    q_ref,
    k_ref,
    v_ref,
    go_ref,
    w_ref,
    link_ref,
    cloud_ref,
    edge_ref,
    out_ref,
    dq_ref,
    dk_ref,
    dv_ref,
    dw_ref,
    w_in,
    kv,
    qg,
    meta,
    stat,
    dof,
    wc,
    at,
    qb,
    gb,
    bias,
    nkv,
    s_buf,
    p_buf,
    low_buf,
    mcol,
    rcol,
    dcol,
    dk_acc,
    dv_acc,
    dwp,
    cs,
    cr,
    xs,
    xr,
    xf,
    zs,
    gx,
    gc,
    send,
    recv,
    local,
):
    strip = lax.axis_index("strip")
    y = lax.axis_index("head")
    core = strip % 2
    z = (strip // 2) % 16
    x = strip // 32
    upper = z // 8

    def at_chip(dx, dz, other=0):
        c = (core + other) % 2
        return (((x + dx + 4) % 4) * 32 + ((z + dz) % 16) * 2 + c, y)

    quad = z // 4

    def near(n):
        return (((x + n // 4) % 4) * 32 + (quad * 4 + (z + n % 4) % 4) * 2 + core, y)

    def near_piece(n):
        return (x + n // 4) % 4 * 4 + (z + n % 4) % 4

    def at_head(dy):
        return (strip, (y + dy) % 4)

    counter = [0]

    def copy(src, dst, device):
        i = counter[0]
        counter[0] += 1
        made = pltpu.make_async_remote_copy(
            src_ref=src,
            dst_ref=dst,
            send_sem=send.at[i],
            recv_sem=recv.at[i],
            device_id=device,
            device_id_type=MESH,
        )
        return made

    peers = [near(n) for n in range(1, 16)]
    peers += [at_chip(0, dz) for dz in (4, 8, 12)]
    peers += [at_chip(dx, 8) for dx in (1, 2, 3)]
    peers += [at_head(dy) for dy in (1, 2, 3)]
    peers += [at_chip(0, 0, 1)]
    barrier = pltpu.get_barrier_semaphore()
    for peer in peers:
        pl.semaphore_signal(barrier, inc=1, device_id=peer, device_id_type=MESH)

    my_columns = pl.ds(pl.multiple_of(y * FEAT, FEAT), FEAT)
    pair = pl.ds(6, 2)
    fills = [pltpu.make_async_copy(go_ref, dof.at[y], local.at[0])]
    fills += [pltpu.make_async_copy(w_ref, w_in, local.at[1])]
    fills += [pltpu.make_async_copy(w_ref.at[:, my_columns], wc.at[y], local.at[2])]
    for g in range(2):
        fills += [pltpu.make_async_copy(q_ref, qg.at[0, g, pair], local.at[3 + g])]
        fills += [pltpu.make_async_copy(k_ref, kv.at[0, g, pair], local.at[5 + g])]
        fills += [pltpu.make_async_copy(v_ref, kv.at[1, g, pair], local.at[7 + g])]
    for made in fills:
        made.start()

    row_id = lax.broadcasted_iota(jnp.int32, (16, BLOCK), 0)
    mine = jnp.zeros((16, BLOCK), jnp.int32)
    member = []
    for g in range(2):
        live = jnp.where(cloud_ref[g] == 0, edge_ref[g], 0)
        mine = jnp.where(row_id == g, live, mine)
        row = []
        for l in range(6):
            has = jnp.int32(0)
            for n in range(4):
                has = has + jnp.where(link_ref[g, n] == l, 1, 0)
            row.append(has)
            mine = jnp.where(row_id == 2 + 6 * g + l, has, mine)
        member.append(row)
    meta[6] = mine

    pl.semaphore_wait(barrier, len(peers))

    own_grad = qg.at[1, 0, pair]
    sources = (k_ref, v_ref, q_ref, own_grad)
    places = [kv.at[0], kv.at[1], qg.at[0], qg.at[1]]
    cross, own, onward = [], [], []
    for src, place in zip(sources, places):
        cross.append([[copy(src.at[g], place.at[g, 2], at_chip(0, 8))] for g in range(2)])
        own.append(
            [copy(src, place.at[:, 1], at_chip(1, 0)), copy(src, place.at[:, 0], at_chip(-1, 0))]
        )
        onward.append(
            [
                [
                    copy(place.at[g, 2], place.at[g, 4], at_chip(1, 0)),
                    copy(place.at[g, 2], place.at[g, 3], at_chip(-1, 0)),
                    copy(place.at[g, 2], place.at[g, 5], at_chip(2, 0)),
                ]
                for g in range(2)
            ]
        )

    def to_far(buf):
        return [
            copy(buf.at[6], buf.at[1], at_chip(1, 0)),
            copy(buf.at[6], buf.at[0], at_chip(-1, 0)),
            copy(buf.at[6], buf.at[2], at_chip(0, 8)),
            copy(buf.at[6], buf.at[4], at_chip(1, 8)),
            copy(buf.at[6], buf.at[3], at_chip(-1, 8)),
            copy(buf.at[6], buf.at[5], at_chip(2, 8)),
        ]

    meta_out = to_far(meta)
    stat_out = to_far(stat)
    y_go = [copy(go_ref, dof.at[y], at_head(dy)) for dy in (1, 2, 3)]
    y_w = [
        copy(
            w_ref.at[:, pl.ds(pl.multiple_of((y + dy) % 4 * FEAT, FEAT), FEAT)],
            wc.at[y],
            at_head(dy),
        )
        for dy in (1, 2, 3)
    ]
    y_at = [copy(at.at[y], at.at[y], at_head(dy)) for dy in (1, 2, 3)]
    c_rs = copy(cs, cr, at_chip(0, 0, 1))
    z_sum = [copy(zs.at[quad], zs.at[quad], at_chip(0, dz)) for dz in (4, 8, 12)]
    def quarter(dx):
        return pl.ds((x - dx + 4) % 4 * 4, 4)

    c_ag = [copy(gx.at[quarter(dx)], gc.at[quarter(dx)], at_chip(0, 0, 1)) for dx in range(4)]
    base = counter[0]

    def near_rs(n):
        return pltpu.make_async_remote_copy(
            src_ref=xs.at[near_piece(n)],
            dst_ref=xr.at[n],
            send_sem=send.at[base + n],
            recv_sem=recv.at[base + n],
            device_id=near(n),
            device_id_type=MESH,
        )

    def near_ag(n):
        return pltpu.make_async_remote_copy(
            src_ref=gx.at[near_piece(0)],
            dst_ref=gx.at[near_piece(0)],
            send_sem=send.at[base + 16 + n],
            recv_sem=recv.at[base + 16 + n],
            device_id=near(n),
            device_id_type=MESH,
        )

    def start(copies):
        for made in copies:
            made.start()

    def arrived(copies):
        for made in copies:
            made.wait_recv()

    def sent(copies):
        for made in copies:
            made.wait_send()

    key, value, query, cot = range(4)
    for g in range(2):
        start(cross[key][g])
    for g in range(2):
        start(cross[value][g])
    start(y_go)
    start(meta_out)

    head_of = lax.broadcasted_iota(jnp.int32, (1, FEAT), 1) // HEAD_DIM
    in_head = [jnp.where(head_of == h, 1.0, 0.0).astype(F32) for h in range(HEADS)]
    in_head_low = [m.astype(BF16) for m in in_head]

    def spread(block):
        return jnp.concatenate([block * m for m in in_head_low], axis=0)

    def gathered(full):
        total = full[:BLOCK] * in_head[0]
        for h in range(1, HEADS):
            total = total + full[h * BLOCK : (h + 1) * BLOCK] * in_head[h]
        return total

    for made in fills:
        made.wait()
    for g in range(2):
        qb[g] = spread(qg[0, 0, 6 + g])

    arrived(y_go)
    grad = nt(dof[0], w_in[:, :FEAT])
    for i in range(1, 4):
        grad = grad + nt(dof[i], w_in[:, i * FEAT : (i + 1) * FEAT])
    grad = grad.astype(BF16)
    for g in range(2):
        for b in range(2):
            qg[1, g, 6 + b] = grad[b * BLOCK : (b + 1) * BLOCK]
        gb[g] = spread(grad[g * BLOCK : (g + 1) * BLOCK])
    start(own[key])
    start(own[value])

    def pass_on(t, g):
        arrived(cross[t][g])
        start(onward[t][g])

    for g in range(2):
        pass_on(key, g)
    for g in range(2):
        start(cross[query][g])

    arrived(meta_out)
    lane = lax.broadcasted_iota(jnp.int32, (1, BLOCK), 1)
    chain = 2 * x + upper
    for g in range(2):
        own_live = jnp.where(cloud_ref[g] == 0, edge_ref[g], 0)
        for j in range(6):
            far = meta[j]
            low_step, high_step = STEPS[j]
            step = jnp.where(upper == 0, low_step, high_step)
            inside = jnp.where((chain + step >= 0) & (chain + step < 8), 1, 0)
            listed = inside * jnp.where(
                upper == 0, member[g][link_of(low_step)], member[g][link_of(high_step)]
            )
            live = far[g : g + 1] * listed
            bias[g, :, j * BLOCK : (j + 1) * BLOCK] = jnp.where(lane < live, 0.0, NEG).astype(F32)
            here_low = 2 + 6 * g + link_of(-low_step)
            here_high = 2 + 6 * g + link_of(-high_step)
            lists_us = jnp.where(
                upper == 0, far[here_low : here_low + 1], far[here_high : here_high + 1]
            )
            nkv[g, j] = lists_us * (inside * own_live)
        for b in range(2):
            live = edge_ref[b] if b == g else jnp.where(cloud_ref[b] == 0, edge_ref[b], 0)
            bias[g, :, (6 + b) * BLOCK : (7 + b) * BLOCK] = jnp.where(lane < live, 0.0, NEG).astype(F32)
            nkv[b, 6 + g] = jnp.full((1, BLOCK), live, jnp.int32)

    CHUNK = 32

    def scores(g):
        keys = kv[0, g].reshape(SLOTS * BLOCK, FEAT)
        s_buf[...] = nt(qb[g], keys)

        def soft(r, _):
            rows = pl.ds(pl.multiple_of(r * CHUNK, CHUNK), CHUNK)
            s = s_buf[rows, :] * SCALE2 + bias[g]
            top = jnp.max(s, axis=1, keepdims=True)
            e = jnp.exp2(s - top)
            inv = 1.0 / jnp.sum(e, axis=1, keepdims=True)
            p = e * inv
            p_buf[g, rows, :] = p
            low_buf[g, rows, :] = p.astype(BF16)
            mcol[g, rows, :] = jnp.broadcast_to(top, (CHUNK, BLOCK))
            rcol[g, rows, :] = jnp.broadcast_to(inv, (CHUNK, BLOCK))
            return 0

        lax.fori_loop(0, HEADS * BLOCK // CHUNK, soft, 0)

    def values(g):
        full = nn(low_buf[g], kv[1, g].reshape(SLOTS * BLOCK, FEAT))
        at[y, g * BLOCK : (g + 1) * BLOCK, :] = gathered(full).astype(BF16)

    pass_on(value, 0)
    for g in range(2):
        start(cross[cot][g])
    pass_on(value, 1)
    start(y_w)
    start(own[query])
    start(own[cot])
    arrived(own[key])
    for g in range(2):
        arrived(onward[key][g])
        scores(g)
    arrived(own[value])
    for g in range(2):
        arrived(onward[value][g])
        values(g)

    start(y_at)
    attn_t = at[y].astype(F32).T.astype(BF16)
    weight_scale = tokens ** (-0.5)
    for i in range(4):
        dwp[i] = nn(attn_t, dof[i]) * weight_scale
    theirs = pl.ds(pl.multiple_of((1 - core) * BLOCK, BLOCK), BLOCK)
    ours = pl.ds(pl.multiple_of(core * BLOCK, BLOCK), BLOCK)
    for i in range(4):
        cs[i] = dwp[i, theirs, :].astype(BF16)
    c_rs.start()

    lane_full = lax.broadcasted_iota(jnp.int32, (BLOCK, BLOCK), 1)

    def correction(g):
        t = qg[1, g, 6 + g].astype(F32) * at[y, g * BLOCK : (g + 1) * BLOCK, :].astype(F32)
        packed = jnp.zeros((BLOCK, BLOCK), F32)
        for h in range(HEADS):
            rows = slice(h * BLOCK, (h + 1) * BLOCK)
            d = jnp.broadcast_to(jnp.sum(t * in_head[h], axis=1, keepdims=True), (BLOCK, BLOCK))
            dcol[g, rows, :] = d
            packed = jnp.where(lane_full == h, mcol[g, rows, :], packed)
            packed = jnp.where(lane_full == HEADS + h, rcol[g, rows, :], packed)
            packed = jnp.where(lane_full == 2 * HEADS + h, d, packed)
        stat[6, g] = packed.T[:16]

    def backward_queries(g):
        keys = kv[0, g].reshape(SLOTS * BLOCK, FEAT)
        s_buf[...] = nt(gb[g], kv[1, g].reshape(SLOTS * BLOCK, FEAT))

        def body(r, _):
            rows = pl.ds(pl.multiple_of(r * CHUNK, CHUNK), CHUNK)
            ds = p_buf[g, rows, :] * (s_buf[rows, :] - dcol[g, rows, 0:1])
            low_buf[g, rows, :] = ds.astype(BF16)
            return 0

        lax.fori_loop(0, HEADS * BLOCK // CHUNK, body, 0)
        full = nn(low_buf[g], keys)
        dq_ref[g] = (gathered(full) * SCALE).astype(BF16)

    row_full = lax.broadcasted_iota(jnp.int32, (BLOCK, BLOCK), 0)

    def keys_step(g, j, slot, group):
        queries, cots = spread(qg[0, g, j]), spread(qg[1, g, j])
        st = nt(kv[0, g, 6 + g], queries)
        dp = nt(kv[1, g, 6 + g], cots)
        off = jnp.where(row_full < nkv[g, j], 0.0, NEG).astype(F32)
        rows = stat[slot, group]
        lows, ds = [], []
        for h in range(HEADS):
            cols = slice(h * BLOCK, (h + 1) * BLOCK)
            top = rows[h : h + 1]
            inv = rows[HEADS + h : HEADS + h + 1]
            d = rows[2 * HEADS + h : 2 * HEADS + h + 1]
            p = jnp.exp2(st[:, cols] * SCALE2 + off - top) * inv
            lows.append(p.astype(BF16))
            ds.append((p * (dp[:, cols] - d)).astype(BF16))
        dv_acc[g] += nn(jnp.concatenate(lows, axis=1), cots)
        dk_acc[g] += nn(jnp.concatenate(ds, axis=1), queries)

    def keys_near(g):
        dv_acc[g] = jnp.zeros((BLOCK, FEAT), F32)
        dk_acc[g] = jnp.zeros((BLOCK, FEAT), F32)

        def body(b, _):
            keys_step(g, 6 + b, 6, b)
            return 0

        lax.fori_loop(0, 2, body, 0)

    def keys_far(g, first, last):
        def body(j, _):
            keys_step(g, j, j, g)
            return 0

        lax.fori_loop(first, last, body, 0)

    def each_near(act):
        def body(n, _):
            act(n)
            return 0

        lax.fori_loop(1, 16, body, 0)

    correction(0)
    correction(1)
    start(stat_out)
    c_rs.wait_recv()
    for i in range(4):
        part = dwp[i, ours, :] + cr[i].astype(F32)
        for r in range(4):
            piece = part[r * 32 : (r + 1) * 32]
            xf[4 * i + r] = piece
            xs[4 * i + r] = piece.astype(BF16)
    each_near(lambda n: near_rs(n).start())
    for g in range(2):
        pass_on(query, g)
    backward_queries(0)

    each_near(lambda n: near_rs(n).wait_recv())
    part = xf[near_piece(0)]
    for n in range(1, 16):
        part = part + xr[n].astype(F32)
    zs[quad] = part.astype(BF16)
    start(z_sum)
    for g in range(2):
        pass_on(cot, g)
    backward_queries(1)

    arrived(y_at)
    arrived(y_w)
    result = nn(at[0], wc[0])
    for i in range(1, 4):
        result = result + nn(at[i], wc[i])
    for b in range(2):
        out_ref[b] = result[b * BLOCK : (b + 1) * BLOCK].astype(BF16)

    arrived(z_sum)
    part = zs[0].astype(F32)
    for i in range(1, 4):
        part = part + zs[i].astype(F32)
    gx[near_piece(0)] = part.astype(BF16)
    each_near(lambda n: near_ag(n).start())

    for g in range(2):
        keys_near(g)
    arrived(stat_out)
    arrived(own[query])
    arrived(own[cot])
    for g in range(2):
        keys_far(g, 0, 2)
    for g in range(2):
        arrived(onward[query][g])
        arrived(onward[cot][g])
        keys_far(g, 2, 6)
        dk_ref[g] = (dk_acc[g] * SCALE).astype(BF16)
        dv_ref[g] = dv_acc[g].astype(BF16)

    for dx in range(4):
        for n in range(max(1, 4 * dx), 4 * dx + 4):
            near_ag(n).wait_recv()
        c_ag[dx].start()

    def assemble(buf, first_row):
        for i in range(4):
            for r in range(4):
                rows = pl.ds(pl.multiple_of(first_row + r * 32, 32), 32)
                dw_ref[rows, i * FEAT : (i + 1) * FEAT] = buf[4 * i + r].astype(F32)

    assemble(gx, core * BLOCK)
    arrived(c_ag)
    assemble(gc, (1 - core) * BLOCK)

    for t in range(4):
        for g in range(2):
            sent(cross[t][g])
            sent(onward[t][g])
        sent(own[t])
    for copies in (meta_out, stat_out, y_go, y_w, y_at, z_sum):
        sent(copies)
    c_rs.wait_send()
    sent(c_ag)
    each_near(lambda n: near_rs(n).wait_send())
    each_near(lambda n: near_ag(n).wait_send())


SEMAPHORES = 128


def hand_over(*refs):
    for src, dst in zip(refs[:5], refs[5:]):
        dst[...] = src[...]


def on_device(
    queries, keys_in, values_in, grad_output, w_output, link_dilation_index, clouds, edge_lengths
):
    tokens = queries.shape[0] * lax.axis_size("strip")
    vmem = pl.BlockSpec(memory_space=pltpu.VMEM)
    smem = pl.BlockSpec(memory_space=pltpu.SMEM)
    shape = (2, BLOCK, FEAT)
    block = jax.ShapeDtypeStruct(shape, BF16)
    anywhere = pl.BlockSpec(memory_space=pl.ANY)
    parts = pl.pallas_call(
        functools.partial(kernel, tokens),
        out_shape=(block, block, block, block, jax.ShapeDtypeStruct((FEAT, 4 * FEAT), F32)),
        in_specs=[anywhere] * 5 + [smem] * 3,
        out_specs=(vmem,) * 5,
        scratch_shapes=[
            pltpu.VMEM((FEAT, 4 * FEAT), BF16),
            pltpu.VMEM((2, 2, SLOTS, BLOCK, FEAT), BF16),
            pltpu.VMEM((2, 2, SLOTS, BLOCK, FEAT), BF16),
            pltpu.VMEM((7, 16, BLOCK), jnp.int32),
            pltpu.VMEM((7, 2, 16, BLOCK), F32),
            pltpu.VMEM((4, TOK, FEAT), BF16),
            pltpu.VMEM((4, FEAT, FEAT), BF16),
            pltpu.VMEM((4, TOK, FEAT), BF16),
            pltpu.VMEM((2, HEADS * BLOCK, FEAT), BF16),
            pltpu.VMEM((2, HEADS * BLOCK, FEAT), BF16),
            pltpu.VMEM((2, 1, SLOTS * BLOCK), F32),
            pltpu.VMEM((2, SLOTS, 1, BLOCK), jnp.int32),
            pltpu.VMEM((HEADS * BLOCK, SLOTS * BLOCK), F32),
            pltpu.VMEM((2, HEADS * BLOCK, SLOTS * BLOCK), F32),
            pltpu.VMEM((2, HEADS * BLOCK, SLOTS * BLOCK), BF16),
            pltpu.VMEM((2, HEADS * BLOCK, BLOCK), F32),
            pltpu.VMEM((2, HEADS * BLOCK, BLOCK), F32),
            pltpu.VMEM((2, HEADS * BLOCK, BLOCK), F32),
            pltpu.VMEM((2, BLOCK, FEAT), F32),
            pltpu.VMEM((2, BLOCK, FEAT), F32),
            pltpu.VMEM((4, FEAT, FEAT), F32),
            pltpu.VMEM((4, BLOCK, FEAT), BF16),
            pltpu.VMEM((4, BLOCK, FEAT), BF16),
            pltpu.VMEM((16, 32, FEAT), BF16),
            pltpu.VMEM((16, 32, FEAT), BF16),
            pltpu.VMEM((16, 32, FEAT), F32),
            pltpu.VMEM((4, 32, FEAT), BF16),
            pltpu.VMEM((16, 32, FEAT), BF16),
            pltpu.VMEM((16, 32, FEAT), BF16),
            pltpu.SemaphoreType.DMA((SEMAPHORES,)),
            pltpu.SemaphoreType.DMA((SEMAPHORES,)),
            pltpu.SemaphoreType.DMA((9,)),
        ],
        compiler_params=pltpu.CompilerParams(
            collective_id=0, has_side_effects=True, vmem_limit_bytes=60 * 2**20
        ),
    )(
        queries.reshape(shape),
        keys_in.reshape(shape),
        values_in.reshape(shape),
        grad_output,
        w_output,
        link_dilation_index,
        clouds,
        edge_lengths,
    )
    result, dq, dk, dv, dw = pl.pallas_call(
        hand_over,
        out_shape=[jax.ShapeDtypeStruct(part.shape, part.dtype) for part in parts],
        in_specs=[vmem] * 5,
        out_specs=[vmem] * 5,
    )(*parts)
    flat = (TOK, FEAT)
    return result.reshape(flat), dq.reshape(flat), dk.reshape(flat), dv.reshape(flat), dw


def solution(mesh):
    return jax.shard_map(
        on_device,
        mesh=mesh,
        in_specs=(
            P("strip", "head"),
            P("strip", "head"),
            P("strip", "head"),
            P("strip", "head"),
            P("head", None),
            P("strip", None),
            P("strip"),
            P("strip"),
        ),
        out_specs=(
            P("strip", "head"),
            P("strip", "head"),
            P("strip", "head"),
            P("strip", "head"),
            P("head", None),
        ),
        check_vma=False,
    )
```
